32 devices in a mesh: groups: 2 (over x), img: 16 (over z, y, core).
Axes of the slice: x: 2, y: 2, z: 4, core: 2. Of those that a mesh axis runs over, the one named last changes fastest.
Arguments:
- descriptors: bfloat16 [64, 384, 256], P(('groups', 'img')), parts along dimension 0, may hold values from -6 to 6
- pair_list: int32 [128, 2], P(('groups', 'img')), parts along dimension 0, may hold values from -1 to 31, as said below
- key_proj: bfloat16 [256, 256], replicated, may hold values from -0.375 to 0.375
- value_proj: bfloat16 [256, 256], replicated, may hold values from -0.375 to 0.375
- out_proj: bfloat16 [256, 256], replicated, may hold values from -0.375 to 0.375
- ffn_first: bfloat16 [512, 512], replicated, may hold values from -0.25 to 0.25
- norm_gain: float32 [512], replicated, may hold values from 0.5 to 1.5
- norm_bias: float32 [512], replicated, may hold values from -3 to 3
- ffn_second: bfloat16 [512, 256], replicated, may hold values from -0.25 to 0.25
Outputs:
- updated: bfloat16 [64, 384, 256], P(('groups', 'img')), parts along dimension 0
The draws below stay inside these ranges and needn't reach their ends.
There are 2 independent parts, one for each index of `groups`. The reference program is written for one: setup_inputs(seed, part) draws one part's arguments, and reference() takes and returns one part's arrays. A program takes and returns all parts, laid end to end along the dimension named above; an argument that names none is the same for every part. Nothing has to cross between parts.
Inputs may be any that keep to these rules, and one draw needn't show every extreme that they name: `pair_list`: rows come in groups of 4, group g on index g of img. In each group the used rows come first, 2 to 4 of them; unused rows hold -1 in both columns. A used row (i, j) has i in images 2 * g to 2 * (g + 1) - 1, j different from i and in images 2 * g to 2 * (g + 3) - 1. Slot s below 2 of group g has i = 2 * g + s. Some group uses all 4 rows and has a second image in group g + 2.
All inputs are finite; a program needn't handle non-finite values.
Results may differ from the reference program's by a relative error of at most 0.0052.
Values may be sent and summed in bfloat16 or wider, within the bound.
A program may use at most 128 MiB of HBM per device.

```python
import math
import jax
import jax.numpy as jnp
from jax import lax

D = 256
HEADS = 4
HID = 512
KEYPTS = 384
IMG_DEV = 2
PAIR_CAP = 4
REACH = 2
IMG = 32
PAIRS = 64


def draw_descriptors(key, part):
    noise_key = jax.random.fold_in(key, 0)
    full_shape = (IMG, KEYPTS, D)
    values = jnp.clip(jax.random.normal(noise_key, full_shape), -6.0, 6.0)
    return values.astype(jnp.bfloat16)


def draw_pair_list(key, part):
    group_count = PAIRS // PAIR_CAP
    split_keys = jax.random.split(key, 5)
    groups = jnp.arange(group_count)
    slot_ids = jnp.arange(PAIR_CAP)
    used = jax.random.randint(split_keys[0], (group_count,), IMG_DEV, PAIR_CAP + 1)
    busiest = jax.random.randint(split_keys[1], (), 0, group_count - REACH)
    used = jnp.where(groups == busiest, PAIR_CAP, used)
    first_local = jax.random.randint(split_keys[2], (group_count, PAIR_CAP), 0, IMG_DEV)
    first_local = jnp.where(slot_ids[None, :] < IMG_DEV, slot_ids[None, :], first_local)
    ahead = jax.random.randint(split_keys[3], (group_count, PAIR_CAP), 0, REACH + 1)
    ahead = jnp.where((groups[:, None] == busiest) & (slot_ids[None, :] == 0), REACH, ahead)
    ahead = jnp.minimum(ahead, group_count - 1 - groups[:, None])
    second_local = jax.random.randint(split_keys[4], (group_count, PAIR_CAP), 0, IMG_DEV)
    first_image = groups[:, None] * IMG_DEV + first_local
    second_image = (groups[:, None] + ahead) * IMG_DEV + second_local
    second_image = jnp.where(second_image == first_image, groups[:, None] * IMG_DEV + (first_local + 1) % IMG_DEV, second_image)
    live = slot_ids[None, :] < used[:, None]
    result = jnp.stack([jnp.where(live, first_image, -1), jnp.where(live, second_image, -1)], axis=-1)
    return result.reshape(PAIRS, 2).astype(jnp.int32)


def scatter_about(rng, extent, scale, bound, dtype=jnp.bfloat16):
    values = scale * jax.random.normal(rng, extent, jnp.float32)
    return jnp.clip(values, min=-bound, max=bound).astype(dtype)


def setup_inputs(seed: int = 0, part: int = 0) -> dict:
    streams_of = jax.random.split(jax.random.key(seed), 10)
    part_splits = jax.random.split(jax.random.fold_in(streams_of[9], part), 10)
    return {
        "descriptors": draw_descriptors(jax.random.fold_in(jax.random.fold_in(streams_of[9], part), 71), part),
        "pair_list": draw_pair_list(jax.random.fold_in(jax.random.fold_in(streams_of[9], part), 71), part),
        "key_proj": scatter_about(streams_of[2], (D, D), D ** -0.5, 0.375),
        "value_proj": scatter_about(streams_of[3], (D, D), D ** -0.5, 0.375),
        "out_proj": scatter_about(streams_of[4], (D, D), D ** -0.5, 0.375),
        "ffn_first": scatter_about(streams_of[5], (HID, HID), HID ** -0.5, 0.25),
        "norm_gain": jnp.clip(1.0 + 0.1 * jax.random.normal(streams_of[6], (HID,), jnp.float32), 0.5, 1.5),
        "norm_bias": scatter_about(streams_of[7], (HID,), 0.5, 3.0, jnp.float32),
        "ffn_second": scatter_about(streams_of[8], (HID, D), HID ** -0.5, 0.25),
    }


EMPTY_MAX = -1e+29

def rounded(values):
    return lax.optimization_barrier(values.astype(jnp.bfloat16)).astype(jnp.float32)

def product(left_side, right_side):
    return jnp.dot(left_side.astype(jnp.float32), right_side.astype(jnp.float32), precision=lax.Precision.HIGHEST)

def pair_pieces(first_keys, first_values, second_keys, second_values):
    head_size = D // HEADS
    score_scale = 1.0 / math.sqrt(head_size)
    row_maxima, row_totals, row_sums = ([], [], [])
    col_maxima, col_totals, col_sums = ([], [], [])
    for h in range(HEADS):
        low_col = h * head_size
        high_col = low_col + head_size
        scores = product(first_keys[:, low_col:high_col], second_keys[:, low_col:high_col].T) * score_scale
        row_max = lax.optimization_barrier(jnp.max(scores, axis=1))
        row_weights = jnp.exp(scores - row_max[:, None])
        row_maxima.append(row_max)
        row_totals.append(lax.optimization_barrier(jnp.sum(row_weights, axis=1)))
        row_sums.append(product(rounded(row_weights), second_values[:, low_col:high_col]))
        col_max = lax.optimization_barrier(jnp.max(scores, axis=0))
        col_weights = jnp.exp(scores - col_max[None, :])
        col_maxima.append(col_max)
        col_totals.append(lax.optimization_barrier(jnp.sum(col_weights, axis=0)))
        col_sums.append(product(rounded(col_weights).T, first_values[:, low_col:high_col]))
    return (jnp.stack(row_maxima), jnp.stack(row_totals), jnp.concatenate(row_sums, axis=1), jnp.stack(col_maxima), jnp.stack(col_totals), jnp.concatenate(col_sums, axis=1))

def scaled_sums(numbers, factors):
    points = numbers.shape[-2]
    shaped = numbers.reshape(numbers.shape[:-2] + (points, HEADS, D // HEADS))
    return (shaped * jnp.swapaxes(factors, -1, -2)[..., None]).reshape(numbers.shape)

def combine(earlier, later):
    early_max, early_den, early_num = earlier
    late_max, late_den, late_num = later
    top_max = jnp.maximum(early_max, late_max)
    early_factor = jnp.exp(early_max - top_max)
    late_factor = jnp.exp(late_max - top_max)
    total_den = early_factor * early_den + late_factor * late_den
    total_num = scaled_sums(early_num, early_factor) + scaled_sums(late_num, late_factor)
    return (top_max, total_den, total_num)

def finish_layer(flat_rows, totals, out_proj, ffn_first, norm_gain, norm_bias, ffn_second):
    maxima, denoms, numers = totals
    images, points, features = numers.shape
    message = numers.reshape(images, points, HEADS, features // HEADS) / jnp.swapaxes(denoms, 1, 2)[..., None]
    message = rounded(message.reshape(images * points, features))
    told = rounded(product(message, out_proj))
    joined = jnp.concatenate([flat_rows.astype(jnp.float32), told], axis=1)
    hidden = product(joined, ffn_first)
    centre = lax.optimization_barrier(jnp.mean(hidden, axis=1, keepdims=True))
    deviation = hidden - centre
    second_moment = lax.optimization_barrier(jnp.mean(deviation * deviation, axis=1, keepdims=True))
    normed = deviation * lax.rsqrt(second_moment + 1e-05) * norm_gain + norm_bias
    active = rounded(jax.nn.gelu(normed, approximate=False))
    return (flat_rows.astype(jnp.float32) + product(active, ffn_second)).astype(jnp.bfloat16)

def reference(descriptors, pair_list, key_proj, value_proj, out_proj, ffn_first, norm_gain, norm_bias, ffn_second):
    images, points, features = descriptors.shape
    flat_rows = descriptors.reshape(images * points, features)
    keys_all = rounded(product(flat_rows, key_proj)).reshape(images, points, features)
    values_all = rounded(product(flat_rows, value_proj)).reshape(images, points, features)
    start = (jnp.full((images, HEADS, points), EMPTY_MAX, jnp.float32), jnp.zeros((images, HEADS, points), jnp.float32), jnp.zeros((images, points, features), jnp.float32))

    def fold_image(totals, image, pieces):
        current = tuple((lax.dynamic_index_in_dim(item, image, 0) for item in totals))
        merged = combine(current, tuple((piece[None] for piece in pieces)))
        return tuple((lax.dynamic_update_index_in_dim(item, new_item, image, 0) for item, new_item in zip(totals, merged)))

    def visit(totals, pair_row):

        def work(running):
            first_image = pair_row[0]
            second_image = pair_row[1]
            pieces = pair_pieces(keys_all[first_image], values_all[first_image], keys_all[second_image], values_all[second_image])
            running = fold_image(running, first_image, pieces[:3])
            return fold_image(running, second_image, pieces[3:])

        def keep(running):
            return running
        return (lax.cond(pair_row[0] >= 0, work, keep, totals), None)
    totals, _ = lax.scan(visit, start, pair_list)
    result = finish_layer(flat_rows, totals, out_proj, ffn_first, norm_gain, norm_bias, ffn_second)
    return result.reshape(images, points, features)
```

```python
import functools
import math

import jax
import jax.numpy as jnp
from jax import lax
from jax.experimental import pallas as pl
from jax.experimental.pallas import tpu as pltpu
from jax.sharding import PartitionSpec as P

HEADS = 4
REACH = 2
WINDOW = 2 * REACH + 1
CHUNKS = 4
FLOW_PARTNER, FLOW_FACING, FLOW_RELAY, FLOW_SHARED = range(4)
ONES_ROWS = 16
VERY_LOW = -1e30
VMEM_BYTES = 48 * 2**20


def project(rows, key_proj, value_proj_t):
    keys = jnp.dot(rows, key_proj, preferred_element_type=jnp.float32)
    values_t = lax.dot_general(
        value_proj_t, rows, (((1,), (1,)), ((), ())), preferred_element_type=jnp.float32
    )
    return keys.astype(jnp.bfloat16), values_t.astype(jnp.bfloat16)


def exchange_kernel(
    device_count,
    own_ref,
    pairs_ref,
    key_proj_ref,
    value_proj_ref,
    keys_ref,
    values_ref,
    lists_ref,
    land,
    land_lists,
    send_sems,
    recv_sems,
):
    img_count, points, features = own_ref.shape
    me = lax.axis_index("img")
    chip = lax.div(me, 2)
    core = lax.rem(me, 2)
    odd = lax.rem(chip, 2)
    chip_count = device_count // 2
    partner = me + 1 - 2 * core
    facing = me + 2 * (1 - 2 * odd)
    relay_to = me + 4 * (1 - 2 * odd)
    relay_from = me - 4 * (1 - 2 * odd)
    gives_relay = (relay_to >= 0) & (relay_to < 2 * chip_count)
    gets_relay = (relay_from >= 0) & (relay_from < 2 * chip_count)
    shares_facing = odd == core
    shares_relay = (odd != core) & gets_relay
    gets_shared = (odd != core) | gets_relay

    land_lists[...] = jnp.full(land_lists.shape, -1, jnp.int32)
    land_lists[0, 0 : pairs_ref.shape[0], 0 : pairs_ref.shape[1]] = pairs_ref[...]

    barrier = pltpu.get_barrier_semaphore()

    def greet(device):
        pl.semaphore_signal(
            barrier, inc=1, device_id={"img": device}, device_id_type=pl.DeviceIdType.MESH
        )

    greet(partner)
    greet(facing)

    @pl.when(gives_relay)
    def _():
        greet(relay_to)

    @pl.when(gets_relay)
    def _():
        greet(relay_from)

    pl.semaphore_wait(
        barrier, 2 + gives_relay.astype(jnp.int32) + gets_relay.astype(jnp.int32)
    )

    pieces = CHUNKS // img_count
    rows = points // pieces

    def transfer(flow, part, source, device):
        if part == CHUNKS:
            src = land_lists.at[source]
            dst = land_lists.at[flow + 1]
        else:
            spot = (part // pieces, pl.ds((part % pieces) * rows, rows))
            src = own_ref.at[spot] if source == 0 else land.at[(source - 1,) + spot]
            dst = land.at[(flow,) + spot]
        return pltpu.make_async_remote_copy(
            src_ref=src,
            dst_ref=dst,
            send_sem=send_sems.at[flow, part],
            recv_sem=recv_sems.at[flow, part],
            device_id={"img": device},
            device_id_type=pl.DeviceIdType.MESH,
        )

    parts = [CHUNKS] + list(range(CHUNKS))
    for part in parts:
        transfer(FLOW_FACING, part, 0, facing).start()
    for part in parts:
        transfer(FLOW_PARTNER, part, 0, partner).start()

    def after_facing(part):
        transfer(FLOW_FACING, part, 0, facing).wait_recv()

        @pl.when(gives_relay)
        def _():
            transfer(FLOW_RELAY, part, 1 + FLOW_FACING, relay_to).start()

        @pl.when(shares_facing)
        def _():
            transfer(FLOW_SHARED, part, 1 + FLOW_FACING, partner).start()

    def after_relay(part):
        @pl.when(gets_relay)
        def _():
            transfer(FLOW_RELAY, part, 1 + FLOW_FACING, relay_from).wait_recv()

        @pl.when(shares_relay)
        def _():
            transfer(FLOW_SHARED, part, 1 + FLOW_RELAY, partner).start()

    value_proj_t = value_proj_ref[...].T
    key_proj = key_proj_ref[...]

    def project_into(place, block_ref):
        for image in range(img_count):
            keys, values_t = project(block_ref[image], key_proj, value_proj_t)
            keys_ref[img_count * place + image] = keys
            values_ref[img_count * place + image] = values_t

    place_partner = REACH + 1 - 2 * core
    place_shared = REACH - 1 + 2 * core
    place_facing = 2 * REACH * (1 - odd)
    place_relay = 2 * REACH * odd

    project_into(REACH, own_ref)
    after_facing(CHUNKS)
    after_facing(0)
    after_relay(CHUNKS)
    for part in parts:
        transfer(FLOW_PARTNER, part, 0, partner).wait_recv()
    for part in range(1, CHUNKS):
        after_facing(part)
        after_relay(part - 1)
        if part == 1:
            project_into(place_partner, land.at[FLOW_PARTNER])
    project_into(place_facing, land.at[FLOW_FACING])
    after_relay(CHUNKS - 1)

    @pl.when(gets_relay)
    def _():
        project_into(place_relay, land.at[FLOW_RELAY])

    @pl.when(gets_shared)
    def _():
        for part in parts:
            transfer(FLOW_SHARED, part, 1 + FLOW_FACING, partner).wait_recv()
        project_into(place_shared, land.at[FLOW_SHARED])

    for part in parts:
        transfer(FLOW_FACING, part, 0, facing).wait_send()
        transfer(FLOW_PARTNER, part, 0, partner).wait_send()

        @pl.when(gives_relay)
        def _():
            transfer(FLOW_RELAY, part, 1 + FLOW_FACING, relay_to).wait_send()

        @pl.when(shares_facing)
        def _():
            transfer(FLOW_SHARED, part, 1 + FLOW_FACING, partner).wait_send()

        @pl.when(shares_relay)
        def _():
            transfer(FLOW_SHARED, part, 1 + FLOW_RELAY, partner).wait_send()

    behind_two = jnp.where(odd == 1, land_lists[1 + FLOW_FACING], land_lists[1 + FLOW_RELAY])
    behind_one = jnp.where(core == 1, land_lists[1 + FLOW_PARTNER], land_lists[1 + FLOW_SHARED])
    first_image = (me - REACH) * img_count
    for place, entries in enumerate((behind_two, behind_one, land_lists[0])):
        lists_ref[place] = jnp.where(entries >= 0, entries - first_image, -1)


def attend_kernel(
    slot_count,
    lists_ref,
    own_ref,
    keys_ref,
    values_ref,
    out_proj_ref,
    ffn_first_ref,
    gain_ref,
    bias_ref,
    ffn_second_ref,
    out_ref,
    queries,
    maxima,
    sums,
    sources,
    counts,
):
    img_count, points, features = own_ref.shape
    head_size = features // HEADS
    first_own = REACH * img_count

    for image in range(img_count):
        counts[image] = 0

    def note(image, source):
        wanted = (image >= first_own) & (image < first_own + img_count)

        @pl.when(wanted)
        def _():
            local = image - first_own
            held = counts[local]
            sources[local, held] = source
            counts[local] = held + 1

    for group in range(REACH + 1):
        for slot in range(slot_count):
            first = lists_ref[group, slot, 0]
            second = lists_ref[group, slot, 1]
            if group == REACH:
                note(first, second)
            note(second, first)

    head_of = lax.broadcasted_iota(jnp.int32, (points, features), 1) // head_size
    ones = jnp.ones((ONES_ROWS, points), jnp.bfloat16)

    @pl.loop(0, img_count)
    def _(image):
        own_keys = keys_ref[first_own + image].astype(jnp.float32) * (1.0 / math.sqrt(head_size))
        for h in range(HEADS):
            queries[h * points : (h + 1) * points] = jnp.where(
                head_of == h, own_keys, 0.0
            ).astype(jnp.bfloat16)
        maxima[...] = jnp.full(maxima.shape, VERY_LOW, jnp.float32)
        sums[...] = jnp.zeros(sums.shape, jnp.float32)

        @pl.loop(0, counts[image])
        def _(index):
            source = sources[image, index]
            keys = keys_ref[source]
            values_t = values_ref[source]
            for h in range(HEADS):
                scores = lax.dot_general(
                    keys,
                    queries[h * points : (h + 1) * points],
                    (((1,), (1,)), ((), ())),
                    preferred_element_type=jnp.float32,
                )
                held_max = maxima[h : h + 1]
                top = jnp.maximum(held_max, jnp.max(scores, axis=0, keepdims=True))
                weights = jnp.exp(scores - top).astype(jnp.bfloat16)
                with_ones = jnp.concatenate(
                    [values_t[h * head_size : (h + 1) * head_size], ones], axis=0
                )
                added = jnp.dot(with_ones, weights, preferred_element_type=jnp.float32)
                sums[h] = sums[h] * jnp.exp(held_max - top) + added
                maxima[h : h + 1] = top

        message = jnp.concatenate(
            [sums[h, :head_size] / sums[h, head_size : head_size + 1] for h in range(HEADS)],
            axis=0,
        )
        message = message.T.astype(jnp.bfloat16)
        told = jnp.dot(message, out_proj_ref[...], preferred_element_type=jnp.float32).astype(
            jnp.bfloat16
        )
        own = own_ref[image]
        hidden = jnp.dot(
            own, ffn_first_ref[:features], preferred_element_type=jnp.float32
        ) + jnp.dot(told, ffn_first_ref[features:], preferred_element_type=jnp.float32)
        centre = jnp.mean(hidden, axis=1, keepdims=True)
        deviation = hidden - centre
        second_moment = jnp.mean(deviation * deviation, axis=1, keepdims=True)
        normed = deviation * lax.rsqrt(second_moment + 1e-05) * gain_ref[...] + bias_ref[...]
        active = 0.5 * normed * (1.0 + lax.erf(normed * math.sqrt(0.5)))
        result = own.astype(jnp.float32) + jnp.dot(
            active.astype(jnp.bfloat16), ffn_second_ref[...], preferred_element_type=jnp.float32
        )
        out_ref[image] = result.astype(jnp.bfloat16)


def shards(
    device_count,
    descriptors,
    pair_list,
    key_proj,
    value_proj,
    out_proj,
    ffn_first,
    norm_gain,
    norm_bias,
    ffn_second,
):
    img_count, points, features = descriptors.shape
    slot_count = pair_list.shape[0]
    window = WINDOW * img_count
    in_vmem = pl.BlockSpec(memory_space=pltpu.VMEM)
    in_smem = pl.BlockSpec(memory_space=pltpu.SMEM)
    keys, values, lists = pl.pallas_call(
        functools.partial(exchange_kernel, device_count),
        out_shape=(
            jax.ShapeDtypeStruct((window, points, features), jnp.bfloat16),
            jax.ShapeDtypeStruct((window, features, points), jnp.bfloat16),
            jax.ShapeDtypeStruct((REACH + 1, 8, 128), jnp.int32),
        ),
        in_specs=[in_vmem] * 4,
        out_specs=(in_vmem, in_vmem, in_vmem),
        scratch_shapes=[
            pltpu.VMEM((4, img_count, points, features), jnp.bfloat16),
            pltpu.VMEM((5, 8, 128), jnp.int32),
            pltpu.SemaphoreType.DMA((4, CHUNKS + 1)),
            pltpu.SemaphoreType.DMA((4, CHUNKS + 1)),
        ],
        compiler_params=pltpu.CompilerParams(
            collective_id=0, has_side_effects=True, vmem_limit_bytes=VMEM_BYTES
        ),
        name="exchange",
    )(descriptors, pair_list, key_proj, value_proj)
    return pl.pallas_call(
        functools.partial(attend_kernel, slot_count),
        out_shape=jax.ShapeDtypeStruct(descriptors.shape, jnp.bfloat16),
        in_specs=[in_smem] + [in_vmem] * 8,
        out_specs=in_vmem,
        scratch_shapes=[
            pltpu.VMEM((HEADS * points, features), jnp.bfloat16),
            pltpu.VMEM((8, points), jnp.float32),
            pltpu.VMEM((HEADS, features // HEADS + ONES_ROWS, points), jnp.float32),
            pltpu.SMEM((img_count, (REACH + 2) * slot_count), jnp.int32),
            pltpu.SMEM((img_count,), jnp.int32),
        ],
        compiler_params=pltpu.CompilerParams(vmem_limit_bytes=VMEM_BYTES),
        name="attend",
    )(
        lists,
        descriptors,
        keys,
        values,
        out_proj,
        ffn_first,
        norm_gain.reshape(1, -1),
        norm_bias.reshape(1, -1),
        ffn_second,
    )


def solution(mesh):
    in_specs = (
        P(("groups", "img"), None, None),
        P(("groups", "img"), None),
        P(),
        P(),
        P(),
        P(),
        P(),
        P(),
        P(),
    )
    out_specs = P(("groups", "img"), None, None)
    return jax.shard_map(
        functools.partial(shards, mesh.shape["img"]),
        mesh=mesh,
        in_specs=in_specs,
        out_specs=out_specs,
        check_vma=False,
    )
```

```python
import functools
import math

import jax
import jax.numpy as jnp
from jax import lax
from jax.experimental import pallas as pl
from jax.experimental.pallas import tpu as pltpu
from jax.sharding import PartitionSpec as P

HEADS = 4
REACH = 2
WINDOW = 2 * REACH + 1
CHUNKS = 8
FLOW_PARTNER, FLOW_FACING, FLOW_RELAY, FLOW_SHARED = range(4)
ONES_ROWS = 16
VERY_LOW = -1e30
VMEM_BYTES = 60 * 2**20


def project(rows, key_proj, value_proj_t):
    keys = jnp.dot(rows, key_proj, preferred_element_type=jnp.float32)
    values_t = lax.dot_general(
        value_proj_t, rows, (((1,), (1,)), ((), ())), preferred_element_type=jnp.float32
    )
    return keys.astype(jnp.bfloat16), values_t.astype(jnp.bfloat16)


def exchange_kernel(
    device_count,
    own_hbm,
    pairs_hbm,
    key_proj_hbm,
    value_proj_hbm,
    keys_hbm,
    values_hbm,
    lists_ref,
    own_ref,
    pairs_ref,
    key_proj_ref,
    value_proj_ref,
    keys_ref,
    values_ref,
    land,
    land_lists,
    fetch_sems,
    store_sems,
    send_sems,
    recv_sems,
):
    img_count, points, features = own_hbm.shape
    me = lax.axis_index("img")
    chip = lax.div(me, 2)
    core = lax.rem(me, 2)
    odd = lax.rem(chip, 2)
    chip_count = device_count // 2
    partner = me + 1 - 2 * core
    facing = me + 2 * (1 - 2 * odd)
    relay_to = me + 4 * (1 - 2 * odd)
    relay_from = me - 4 * (1 - 2 * odd)
    gives_relay = (relay_to >= 0) & (relay_to < 2 * chip_count)
    gets_relay = (relay_from >= 0) & (relay_from < 2 * chip_count)
    shares_facing = odd == core
    shares_relay = (odd != core) & gets_relay
    gets_shared = (odd != core) | gets_relay

    fetches = [
        pltpu.make_async_copy(source, target, fetch_sems.at[index])
        for index, (source, target) in enumerate(
            (
                (pairs_hbm, pairs_ref),
                (own_hbm, own_ref),
                (key_proj_hbm, key_proj_ref),
                (value_proj_hbm, value_proj_ref),
            )
        )
    ]
    for fetch in fetches:
        fetch.start()
    land_lists[...] = jnp.full(land_lists.shape, -1, jnp.int32)

    barrier = pltpu.get_barrier_semaphore()

    def greet(device):
        pl.semaphore_signal(
            barrier, inc=1, device_id={"img": device}, device_id_type=pl.DeviceIdType.MESH
        )

    greet(partner)
    greet(facing)

    @pl.when(gives_relay)
    def _():
        greet(relay_to)

    @pl.when(gets_relay)
    def _():
        greet(relay_from)

    pl.semaphore_wait(
        barrier, 2 + gives_relay.astype(jnp.int32) + gets_relay.astype(jnp.int32)
    )

    pieces = CHUNKS // img_count
    rows = points // pieces

    def transfer(flow, part, source, device):
        if part == CHUNKS:
            src = land_lists.at[source]
            dst = land_lists.at[flow + 1]
        else:
            spot = (part // pieces, pl.ds((part % pieces) * rows, rows))
            src = own_hbm.at[spot] if source == 0 else land.at[(source - 1,) + spot]
            dst = land.at[(flow,) + spot]
        return pltpu.make_async_remote_copy(
            src_ref=src,
            dst_ref=dst,
            send_sem=send_sems.at[flow, part],
            recv_sem=recv_sems.at[flow, part],
            device_id={"img": device},
            device_id_type=pl.DeviceIdType.MESH,
        )

    parts = list(range(CHUNKS)) + [CHUNKS]
    for part in range(CHUNKS):
        transfer(FLOW_FACING, part, 0, facing).start()
    for part in range(CHUNKS):
        transfer(FLOW_PARTNER, part, 0, partner).start()
    fetches[0].wait()
    land_lists[0, 0 : pairs_ref.shape[0], 0 : pairs_ref.shape[1]] = pairs_ref[...]
    transfer(FLOW_FACING, CHUNKS, 0, facing).start()
    transfer(FLOW_PARTNER, CHUNKS, 0, partner).start()
    for fetch in fetches[1:]:
        fetch.wait()

    def after_facing(part):
        transfer(FLOW_FACING, part, 0, facing).wait_recv()

        @pl.when(gives_relay)
        def _():
            transfer(FLOW_RELAY, part, 1 + FLOW_FACING, relay_to).start()

        @pl.when(shares_facing)
        def _():
            transfer(FLOW_SHARED, part, 1 + FLOW_FACING, partner).start()

    def after_relay(part):
        @pl.when(gets_relay)
        def _():
            transfer(FLOW_RELAY, part, 1 + FLOW_FACING, relay_from).wait_recv()

        @pl.when(shares_relay)
        def _():
            transfer(FLOW_SHARED, part, 1 + FLOW_RELAY, partner).start()

    value_proj_t = value_proj_ref[...].T
    key_proj = key_proj_ref[...]

    def stores(slot, place, image):
        return [
            pltpu.make_async_copy(
                source.at[img_count * slot + image],
                target.at[img_count * place + image],
                store_sems.at[img_count * slot + image, index],
            )
            for index, (source, target) in enumerate(
                ((keys_ref, keys_hbm), (values_ref, values_hbm))
            )
        ]

    def project_image(slot, place, block_ref, image):
        keys, values_t = project(block_ref[image], key_proj, value_proj_t)
        keys_ref[img_count * slot + image] = keys
        values_ref[img_count * slot + image] = values_t
        for store in stores(slot, place, image):
            store.start()

    place_partner = REACH + 1 - 2 * core
    place_shared = REACH - 1 + 2 * core
    place_facing = 2 * REACH * (1 - odd)
    place_relay = 2 * REACH * odd

    def take_partner(image):
        for part in range(image * pieces, (image + 1) * pieces):
            transfer(FLOW_PARTNER, part, 0, partner).wait_recv()
        project_image(1 + FLOW_PARTNER, place_partner, land.at[FLOW_PARTNER], image)

    def take_relay(image):
        @pl.when(gets_relay)
        def _():
            project_image(1 + FLOW_RELAY, place_relay, land.at[FLOW_RELAY], image)

    def take_shared(image):
        @pl.when(gets_shared)
        def _():
            for part in range(image * pieces, (image + 1) * pieces):
                transfer(FLOW_SHARED, part, 1 + FLOW_FACING, partner).wait_recv()
            project_image(1 + FLOW_SHARED, place_shared, land.at[FLOW_SHARED], image)

    meanwhile = {}
    for image in range(img_count):
        meanwhile.setdefault(image, []).append(functools.partial(take_partner, image))
        if image + 1 < img_count:
            done = (image + 1) * pieces
            meanwhile.setdefault(done - 1, []).append(
                functools.partial(
                    project_image, 1 + FLOW_FACING, place_facing, land.at[FLOW_FACING], image
                )
            )
            meanwhile.setdefault(done, []).append(functools.partial(take_relay, image))
            meanwhile.setdefault(done + 1, []).append(functools.partial(take_shared, image))

    for image in range(img_count):
        project_image(0, REACH, own_ref, image)
    for part in range(CHUNKS):
        after_facing(part)
        if part >= 1:
            after_relay(part - 1)
        for step in meanwhile.get(part, []):
            step()
    after_facing(CHUNKS)
    transfer(FLOW_PARTNER, CHUNKS, 0, partner).wait_recv()
    project_image(1 + FLOW_FACING, place_facing, land.at[FLOW_FACING], img_count - 1)
    after_relay(CHUNKS - 1)
    after_relay(CHUNKS)
    take_relay(img_count - 1)
    take_shared(img_count - 1)

    @pl.when(gets_shared)
    def _():
        transfer(FLOW_SHARED, CHUNKS, 1 + FLOW_FACING, partner).wait_recv()

    for part in parts:
        transfer(FLOW_FACING, part, 0, facing).wait_send()
        transfer(FLOW_PARTNER, part, 0, partner).wait_send()

        @pl.when(gives_relay)
        def _():
            transfer(FLOW_RELAY, part, 1 + FLOW_FACING, relay_to).wait_send()

        @pl.when(shares_facing)
        def _():
            transfer(FLOW_SHARED, part, 1 + FLOW_FACING, partner).wait_send()

        @pl.when(shares_relay)
        def _():
            transfer(FLOW_SHARED, part, 1 + FLOW_RELAY, partner).wait_send()

    for image in range(img_count):
        for slot, place in (
            (0, REACH),
            (1 + FLOW_PARTNER, place_partner),
            (1 + FLOW_FACING, place_facing),
        ):
            for store in stores(slot, place, image):
                store.wait()

        @pl.when(gets_relay)
        def _():
            for store in stores(1 + FLOW_RELAY, place_relay, image):
                store.wait()

        @pl.when(gets_shared)
        def _():
            for store in stores(1 + FLOW_SHARED, place_shared, image):
                store.wait()

    behind_two = jnp.where(odd == 1, land_lists[1 + FLOW_FACING], land_lists[1 + FLOW_RELAY])
    behind_one = jnp.where(core == 1, land_lists[1 + FLOW_PARTNER], land_lists[1 + FLOW_SHARED])
    first_image = (me - REACH) * img_count
    for place, entries in enumerate((behind_two, behind_one, land_lists[0])):
        lists_ref[place] = jnp.where(entries >= 0, entries - first_image, -1)


def attend_kernel(
    slot_count,
    lists_ref,
    keys_hbm,
    values_hbm,
    own_hbm,
    out_proj_hbm,
    ffn_first_hbm,
    gain_hbm,
    bias_hbm,
    ffn_second_hbm,
    out_ref,
    keys_ref,
    values_ref,
    own_ref,
    out_proj_ref,
    ffn_first_ref,
    gain_ref,
    bias_ref,
    ffn_second_ref,
    queries,
    maxima,
    sums,
    repeats,
    sources,
    counts,
    fetch_sems,
):
    img_count, points, features = own_ref.shape
    head_size = features // HEADS
    window = keys_ref.shape[0]
    first_own = REACH * img_count

    fetches = [
        pltpu.make_async_copy(source, target, fetch_sems.at[index])
        for index, (source, target) in enumerate(
            (
                (keys_hbm, keys_ref),
                (values_hbm, values_ref),
                (own_hbm, own_ref),
                (out_proj_hbm, out_proj_ref),
                (ffn_first_hbm, ffn_first_ref),
                (gain_hbm, gain_ref),
                (bias_hbm, bias_ref),
                (ffn_second_hbm, ffn_second_ref),
            )
        )
    ]
    for fetch in fetches:
        fetch.start()

    for local in range(img_count):
        for source in range(window):
            repeats[local, source] = 0

    def note(image, source):
        wanted = (image >= first_own) & (image < first_own + img_count)

        @pl.when(wanted)
        def _():
            local = image - first_own
            repeats[local, source] = repeats[local, source] + 1

    for group in range(REACH + 1):
        for slot in range(slot_count):
            first = lists_ref[group, 0, slot]
            second = lists_ref[group, 1, slot]
            if group == REACH:
                note(first, second)
            note(second, first)

    for local in range(img_count):
        held = jnp.int32(0)
        for source in range(window):
            sources[local, held] = source
            held = held + (repeats[local, source] > 0).astype(jnp.int32)
        counts[local] = held

    for fetch in fetches[:2]:
        fetch.wait()

    head_of = lax.broadcasted_iota(jnp.int32, (points, features), 1) // head_size
    ones = jnp.ones((ONES_ROWS, points), jnp.bfloat16)

    @pl.loop(0, img_count)
    def _(image):
        own_keys = keys_ref[first_own + image].astype(jnp.float32) * (1.0 / math.sqrt(head_size))
        for h in range(HEADS):
            queries[h * points : (h + 1) * points] = jnp.where(
                head_of == h, own_keys, 0.0
            ).astype(jnp.bfloat16)
        maxima[...] = jnp.full(maxima.shape, VERY_LOW, jnp.float32)
        sums[...] = jnp.zeros(sums.shape, jnp.float32)

        @pl.loop(0, counts[image])
        def _(index):
            source = sources[image, index]
            times = repeats[image, source].astype(jnp.float32)
            keys = keys_ref[source]
            values_t = values_ref[source]
            for pair in range(HEADS // 2):
                scores = lax.dot_general(
                    keys,
                    queries[2 * pair * points : 2 * (pair + 1) * points],
                    (((1,), (1,)), ((), ())),
                    preferred_element_type=jnp.float32,
                )
                held_max = maxima[pair : pair + 1]
                top = jnp.maximum(held_max, jnp.max(scores, axis=0, keepdims=True))
                weights = jnp.exp(scores - top).astype(jnp.bfloat16)
                decay = jnp.exp(held_max - top)
                maxima[pair : pair + 1] = top
                for side in range(2):
                    h = 2 * pair + side
                    with_ones = jnp.concatenate(
                        [values_t[h * head_size : (h + 1) * head_size], ones], axis=0
                    )
                    span = slice(side * points, (side + 1) * points)
                    added = jnp.dot(
                        with_ones, weights[:, span], preferred_element_type=jnp.float32
                    )
                    sums[h] = sums[h] * decay[:, span] + added * times

        @pl.when(image == 0)
        def _():
            for fetch in fetches[2:]:
                fetch.wait()

        message = jnp.concatenate(
            [sums[h, :head_size] / sums[h, head_size : head_size + 1] for h in range(HEADS)],
            axis=0,
        )
        message = message.T.astype(jnp.bfloat16)
        told = jnp.dot(message, out_proj_ref[...], preferred_element_type=jnp.float32).astype(
            jnp.bfloat16
        )
        own = own_ref[image]
        hidden = jnp.dot(
            own, ffn_first_ref[:features], preferred_element_type=jnp.float32
        ) + jnp.dot(told, ffn_first_ref[features:], preferred_element_type=jnp.float32)
        centre = jnp.mean(hidden, axis=1, keepdims=True)
        deviation = hidden - centre
        second_moment = jnp.mean(deviation * deviation, axis=1, keepdims=True)
        normed = deviation * lax.rsqrt(second_moment + 1e-05) * gain_ref[...] + bias_ref[...]
        active = 0.5 * normed * (1.0 + lax.erf(normed * math.sqrt(0.5)))
        result = own.astype(jnp.float32) + jnp.dot(
            active.astype(jnp.bfloat16), ffn_second_ref[...], preferred_element_type=jnp.float32
        )
        out_ref[image] = result.astype(jnp.bfloat16)


def shards(
    device_count,
    descriptors,
    pair_list,
    key_proj,
    value_proj,
    out_proj,
    ffn_first,
    norm_gain,
    norm_bias,
    ffn_second,
):
    img_count, points, features = descriptors.shape
    slot_count = pair_list.shape[0]
    window = WINDOW * img_count
    in_vmem = pl.BlockSpec(memory_space=pltpu.VMEM)
    in_smem = pl.BlockSpec(memory_space=pltpu.SMEM)
    in_hbm = pl.BlockSpec(memory_space=pltpu.HBM)
    keys, values, lists = pl.pallas_call(
        functools.partial(exchange_kernel, device_count),
        out_shape=(
            jax.ShapeDtypeStruct((window, points, features), jnp.bfloat16),
            jax.ShapeDtypeStruct((window, features, points), jnp.bfloat16),
            jax.ShapeDtypeStruct((REACH + 1, 8, 128), jnp.int32),
        ),
        in_specs=[in_hbm] * 4,
        out_specs=(in_hbm, in_hbm, in_vmem),
        scratch_shapes=[
            pltpu.VMEM(descriptors.shape, jnp.bfloat16),
            pltpu.VMEM(pair_list.shape[::-1], jnp.int32),
            pltpu.VMEM(key_proj.shape, jnp.bfloat16),
            pltpu.VMEM(value_proj.shape, jnp.bfloat16),
            pltpu.VMEM((window, points, features), jnp.bfloat16),
            pltpu.VMEM((window, features, points), jnp.bfloat16),
            pltpu.VMEM((4, img_count, points, features), jnp.bfloat16),
            pltpu.VMEM((5, 8, 128), jnp.int32),
            pltpu.SemaphoreType.DMA((4,)),
            pltpu.SemaphoreType.DMA((window, 2)),
            pltpu.SemaphoreType.DMA((4, CHUNKS + 1)),
            pltpu.SemaphoreType.DMA((4, CHUNKS + 1)),
        ],
        compiler_params=pltpu.CompilerParams(
            collective_id=0, has_side_effects=True, vmem_limit_bytes=VMEM_BYTES
        ),
        name="exchange",
    )(descriptors, pair_list.T, key_proj, value_proj)
    return pl.pallas_call(
        functools.partial(attend_kernel, slot_count),
        out_shape=jax.ShapeDtypeStruct(descriptors.shape, jnp.bfloat16),
        in_specs=[in_smem] + [in_hbm] * 8,
        out_specs=in_vmem,
        scratch_shapes=[
            pltpu.VMEM(keys.shape, jnp.bfloat16),
            pltpu.VMEM(values.shape, jnp.bfloat16),
            pltpu.VMEM(descriptors.shape, jnp.bfloat16),
            pltpu.VMEM(out_proj.shape, jnp.bfloat16),
            pltpu.VMEM(ffn_first.shape, jnp.bfloat16),
            pltpu.VMEM((1,) + norm_gain.shape, jnp.float32),
            pltpu.VMEM((1,) + norm_bias.shape, jnp.float32),
            pltpu.VMEM(ffn_second.shape, jnp.bfloat16),
            pltpu.VMEM((HEADS * points, features), jnp.bfloat16),
            pltpu.VMEM((8, 2 * points), jnp.float32),
            pltpu.VMEM((HEADS, features // HEADS + ONES_ROWS, points), jnp.float32),
            pltpu.SMEM((img_count, window), jnp.int32),
            pltpu.SMEM((img_count, window + 1), jnp.int32),
            pltpu.SMEM((img_count,), jnp.int32),
            pltpu.SemaphoreType.DMA((8,)),
        ],
        compiler_params=pltpu.CompilerParams(vmem_limit_bytes=VMEM_BYTES),
        name="attend",
    )(
        lists,
        keys,
        values,
        descriptors,
        out_proj,
        ffn_first,
        norm_gain.reshape(1, -1),
        norm_bias.reshape(1, -1),
        ffn_second,
    )


def solution(mesh):
    in_specs = (
        P(("groups", "img"), None, None),
        P(("groups", "img"), None),
        P(),
        P(),
        P(),
        P(),
        P(),
        P(),
        P(),
    )
    out_specs = P(("groups", "img"), None, None)
    return jax.shard_map(
        functools.partial(shards, mesh.shape["img"]),
        mesh=mesh,
        in_specs=in_specs,
        out_specs=out_specs,
        check_vma=False,
    )
```

```python
import functools
import math

import jax
import jax.numpy as jnp
from jax import lax
from jax.experimental import pallas as pl
from jax.experimental.pallas import tpu as pltpu
from jax.sharding import PartitionSpec as P

HEADS = 4
REACH = 2
WINDOW = 2 * REACH + 1
CHUNKS = 8
LAG = 4
FLOW_PARTNER, FLOW_FACING, FLOW_RELAY, FLOW_SHARED = range(4)
ONES_ROWS = 16
VERY_LOW = -1e30
VMEM_BYTES = 60 * 2**20


def project(rows, key_proj, value_proj_t):
    keys = jnp.dot(rows, key_proj, preferred_element_type=jnp.float32)
    values_t = lax.dot_general(
        value_proj_t, rows, (((1,), (1,)), ((), ())), preferred_element_type=jnp.float32
    )
    return keys.astype(jnp.bfloat16), values_t.astype(jnp.bfloat16)


def exchange_kernel(
    device_count,
    own_hbm,
    pairs_hbm,
    key_proj_hbm,
    value_proj_hbm,
    keys_hbm,
    values_hbm,
    lists_ref,
    own_ref,
    pairs_ref,
    key_proj_ref,
    value_proj_ref,
    keys_ref,
    values_ref,
    land,
    land_lists,
    fetch_sems,
    store_sems,
    send_sems,
    recv_sems,
):
    img_count, points, features = own_hbm.shape
    me = lax.axis_index("img")
    chip = lax.div(me, 2)
    core = lax.rem(me, 2)
    odd = lax.rem(chip, 2)
    chip_count = device_count // 2
    partner = me + 1 - 2 * core
    facing = me + 2 * (1 - 2 * odd)
    relay_to = me + 4 * (1 - 2 * odd)
    relay_from = me - 4 * (1 - 2 * odd)
    gives_relay = (relay_to >= 0) & (relay_to < 2 * chip_count)
    gets_relay = (relay_from >= 0) & (relay_from < 2 * chip_count)
    shares_facing = odd == core
    shares_relay = (odd != core) & gets_relay
    gets_shared = (odd != core) | gets_relay

    fetches = [
        pltpu.make_async_copy(source, target, fetch_sems.at[index])
        for index, (source, target) in enumerate(
            (
                (pairs_hbm, pairs_ref),
                (own_hbm, own_ref),
                (key_proj_hbm, key_proj_ref),
                (value_proj_hbm, value_proj_ref),
            )
        )
    ]
    for fetch in fetches:
        fetch.start()
    land_lists[...] = jnp.full(land_lists.shape, -1, jnp.int32)

    barrier = pltpu.get_barrier_semaphore()

    def greet(device):
        pl.semaphore_signal(
            barrier, inc=1, device_id={"img": device}, device_id_type=pl.DeviceIdType.MESH
        )

    greet(partner)
    greet(facing)

    @pl.when(gives_relay)
    def _():
        greet(relay_to)

    @pl.when(gets_relay)
    def _():
        greet(relay_from)

    pl.semaphore_wait(
        barrier, 2 + gives_relay.astype(jnp.int32) + gets_relay.astype(jnp.int32)
    )

    pieces = CHUNKS // img_count
    rows = points // pieces

    def transfer(flow, part, source, device):
        if part == CHUNKS:
            src = land_lists.at[source]
            dst = land_lists.at[flow + 1]
        else:
            spot = (part // pieces, pl.ds((part % pieces) * rows, rows))
            src = own_hbm.at[spot] if source == 0 else land.at[(source - 1,) + spot]
            dst = land.at[(flow,) + spot]
        return pltpu.make_async_remote_copy(
            src_ref=src,
            dst_ref=dst,
            send_sem=send_sems.at[flow, part],
            recv_sem=recv_sems.at[flow, part],
            device_id={"img": device},
            device_id_type=pl.DeviceIdType.MESH,
        )

    parts = list(range(CHUNKS)) + [CHUNKS]
    for part in range(CHUNKS):
        transfer(FLOW_FACING, part, 0, facing).start()
    for part in range(CHUNKS):
        transfer(FLOW_PARTNER, part, 0, partner).start()
    fetches[0].wait()
    land_lists[0, 0 : pairs_ref.shape[0], 0 : pairs_ref.shape[1]] = pairs_ref[...]
    transfer(FLOW_FACING, CHUNKS, 0, facing).start()
    transfer(FLOW_PARTNER, CHUNKS, 0, partner).start()
    for fetch in fetches[1:]:
        fetch.wait()

    def after_facing(part):
        transfer(FLOW_FACING, part, 0, facing).wait_recv()

        @pl.when(gives_relay)
        def _():
            transfer(FLOW_RELAY, part, 1 + FLOW_FACING, relay_to).start()

        @pl.when(shares_facing)
        def _():
            transfer(FLOW_SHARED, part, 1 + FLOW_FACING, partner).start()

    def after_relay(part):
        @pl.when(gets_relay)
        def _():
            transfer(FLOW_RELAY, part, 1 + FLOW_FACING, relay_from).wait_recv()

        @pl.when(shares_relay)
        def _():
            transfer(FLOW_SHARED, part, 1 + FLOW_RELAY, partner).start()

    value_proj_t = value_proj_ref[...].T
    key_proj = key_proj_ref[...]

    def stores(slot, place, image):
        return [
            pltpu.make_async_copy(
                source.at[img_count * slot + image],
                target.at[img_count * place + image],
                store_sems.at[img_count * slot + image, index],
            )
            for index, (source, target) in enumerate(
                ((keys_ref, keys_hbm), (values_ref, values_hbm))
            )
        ]

    def project_image(slot, place, block_ref, image):
        keys, values_t = project(block_ref[image], key_proj, value_proj_t)
        keys_ref[img_count * slot + image] = keys
        values_ref[img_count * slot + image] = values_t
        for store in stores(slot, place, image):
            store.start()

    place_partner = REACH + 1 - 2 * core
    place_shared = REACH - 1 + 2 * core
    place_facing = 2 * REACH * (1 - odd)
    place_relay = 2 * REACH * odd

    def take_partner(image):
        for part in range(image * pieces, (image + 1) * pieces):
            transfer(FLOW_PARTNER, part, 0, partner).wait_recv()
        project_image(1 + FLOW_PARTNER, place_partner, land.at[FLOW_PARTNER], image)

    def take_relay(image):
        @pl.when(gets_relay)
        def _():
            project_image(1 + FLOW_RELAY, place_relay, land.at[FLOW_RELAY], image)

    def take_shared(image):
        @pl.when(gets_shared)
        def _():
            for part in range(image * pieces, (image + 1) * pieces):
                transfer(FLOW_SHARED, part, 1 + FLOW_FACING, partner).wait_recv()
            project_image(1 + FLOW_SHARED, place_shared, land.at[FLOW_SHARED], image)

    meanwhile = {}
    for image in range(img_count):
        meanwhile.setdefault(image, []).append(functools.partial(take_partner, image))
        if image + 1 < img_count:
            done = (image + 1) * pieces
            meanwhile.setdefault(done - 1, []).append(
                functools.partial(
                    project_image, 1 + FLOW_FACING, place_facing, land.at[FLOW_FACING], image
                )
            )
            meanwhile.setdefault(done - 1 + LAG, []).append(
                functools.partial(take_relay, image)
            )
            meanwhile.setdefault(done + LAG, []).append(functools.partial(take_shared, image))

    for image in range(img_count):
        project_image(0, REACH, own_ref, image)
    for step in range(CHUNKS + LAG):
        if step < CHUNKS:
            after_facing(step)
        if step >= LAG:
            after_relay(step - LAG)
        for task in meanwhile.get(step, []):
            task()
        if step == CHUNKS - 1:
            after_facing(CHUNKS)
            transfer(FLOW_PARTNER, CHUNKS, 0, partner).wait_recv()
            project_image(1 + FLOW_FACING, place_facing, land.at[FLOW_FACING], img_count - 1)
    after_relay(CHUNKS)
    take_relay(img_count - 1)
    take_shared(img_count - 1)

    @pl.when(gets_shared)
    def _():
        transfer(FLOW_SHARED, CHUNKS, 1 + FLOW_FACING, partner).wait_recv()

    for part in parts:
        transfer(FLOW_FACING, part, 0, facing).wait_send()
        transfer(FLOW_PARTNER, part, 0, partner).wait_send()

        @pl.when(gives_relay)
        def _():
            transfer(FLOW_RELAY, part, 1 + FLOW_FACING, relay_to).wait_send()

        @pl.when(shares_facing)
        def _():
            transfer(FLOW_SHARED, part, 1 + FLOW_FACING, partner).wait_send()

        @pl.when(shares_relay)
        def _():
            transfer(FLOW_SHARED, part, 1 + FLOW_RELAY, partner).wait_send()

    for image in range(img_count):
        for slot, place in (
            (0, REACH),
            (1 + FLOW_PARTNER, place_partner),
            (1 + FLOW_FACING, place_facing),
        ):
            for store in stores(slot, place, image):
                store.wait()

        @pl.when(gets_relay)
        def _():
            for store in stores(1 + FLOW_RELAY, place_relay, image):
                store.wait()

        @pl.when(gets_shared)
        def _():
            for store in stores(1 + FLOW_SHARED, place_shared, image):
                store.wait()

    behind_two = jnp.where(odd == 1, land_lists[1 + FLOW_FACING], land_lists[1 + FLOW_RELAY])
    behind_one = jnp.where(core == 1, land_lists[1 + FLOW_PARTNER], land_lists[1 + FLOW_SHARED])
    first_image = (me - REACH) * img_count
    for place, entries in enumerate((behind_two, behind_one, land_lists[0])):
        lists_ref[place] = jnp.where(entries >= 0, entries - first_image, -1)


def attend_kernel(
    slot_count,
    lists_ref,
    keys_hbm,
    values_hbm,
    own_hbm,
    out_proj_hbm,
    ffn_first_hbm,
    gain_hbm,
    bias_hbm,
    ffn_second_hbm,
    out_ref,
    keys_ref,
    values_ref,
    own_ref,
    out_proj_ref,
    ffn_first_ref,
    gain_ref,
    bias_ref,
    ffn_second_ref,
    queries,
    maxima,
    sums,
    repeats,
    sources,
    counts,
    arrived,
    fetch_sems,
    load_sems,
):
    img_count, points, features = own_ref.shape
    head_size = features // HEADS
    window = keys_ref.shape[0]
    first_own = REACH * img_count

    fetches = [
        pltpu.make_async_copy(source, target, fetch_sems.at[index])
        for index, (source, target) in enumerate(
            (
                (own_hbm, own_ref),
                (out_proj_hbm, out_proj_ref),
                (ffn_first_hbm, ffn_first_ref),
                (gain_hbm, gain_ref),
                (bias_hbm, bias_ref),
                (ffn_second_hbm, ffn_second_ref),
            )
        )
    ]

    def loads(source):
        return [
            pltpu.make_async_copy(held.at[source], to.at[source], load_sems.at[source, index])
            for index, (held, to) in enumerate(((keys_hbm, keys_ref), (values_hbm, values_ref)))
        ]

    for local in range(img_count):
        for load in loads(first_own + local):
            load.start()

    for local in range(img_count):
        for source in range(window):
            repeats[local, source] = 0

    def note(image, source):
        wanted = (image >= first_own) & (image < first_own + img_count)

        @pl.when(wanted)
        def _():
            local = image - first_own
            repeats[local, source] = repeats[local, source] + 1

    for group in range(REACH + 1):
        for slot in range(slot_count):
            first = lists_ref[group, 0, slot]
            second = lists_ref[group, 1, slot]
            if group == REACH:
                note(first, second)
            note(second, first)

    for local in range(img_count):
        held = jnp.int32(0)
        for source in range(window):
            sources[local, held] = source
            held = held + (repeats[local, source] > 0).astype(jnp.int32)
        counts[local] = held

    for source in range(window):
        is_own = first_own <= source < first_own + img_count
        arrived[source] = int(is_own)
        if not is_own:
            used = repeats[0, source]
            for local in range(1, img_count):
                used = used + repeats[local, source]

            @pl.when(used > 0)
            def _():
                for load in loads(source):
                    load.start()

    for fetch in fetches:
        fetch.start()
    for local in range(img_count):
        for load in loads(first_own + local):
            load.wait()

    head_of = lax.broadcasted_iota(jnp.int32, (points, features), 1) // head_size
    ones = jnp.ones((ONES_ROWS, points), jnp.bfloat16)

    @pl.loop(0, img_count)
    def _(image):
        own_keys = keys_ref[first_own + image].astype(jnp.float32) * (1.0 / math.sqrt(head_size))
        for h in range(HEADS):
            queries[h * points : (h + 1) * points] = jnp.where(
                head_of == h, own_keys, 0.0
            ).astype(jnp.bfloat16)
        maxima[...] = jnp.full(maxima.shape, VERY_LOW, jnp.float32)
        sums[...] = jnp.zeros(sums.shape, jnp.float32)

        @pl.loop(0, counts[image])
        def _(index):
            source = sources[image, index]

            @pl.when(arrived[source] == 0)
            def _():
                for load in loads(source):
                    load.wait()
                arrived[source] = 1

            times = repeats[image, source].astype(jnp.float32)
            keys = keys_ref[source]
            values_t = values_ref[source]
            for pair in range(HEADS // 2):
                scores = lax.dot_general(
                    keys,
                    queries[2 * pair * points : 2 * (pair + 1) * points],
                    (((1,), (1,)), ((), ())),
                    preferred_element_type=jnp.float32,
                )
                held_max = maxima[pair : pair + 1]
                top = jnp.maximum(held_max, jnp.max(scores, axis=0, keepdims=True))
                weights = jnp.exp((scores - top).astype(jnp.bfloat16))
                decay = jnp.exp(held_max - top)
                maxima[pair : pair + 1] = top
                for side in range(2):
                    h = 2 * pair + side
                    with_ones = jnp.concatenate(
                        [values_t[h * head_size : (h + 1) * head_size], ones], axis=0
                    )
                    span = slice(side * points, (side + 1) * points)
                    added = jnp.dot(
                        with_ones, weights[:, span], preferred_element_type=jnp.float32
                    )
                    sums[h] = sums[h] * decay[:, span] + added * times

        @pl.when(image == 0)
        def _():
            for fetch in fetches:
                fetch.wait()

        message = jnp.concatenate(
            [sums[h, :head_size] / sums[h, head_size : head_size + 1] for h in range(HEADS)],
            axis=0,
        )
        message = message.T.astype(jnp.bfloat16)
        told = jnp.dot(message, out_proj_ref[...], preferred_element_type=jnp.float32).astype(
            jnp.bfloat16
        )
        own = own_ref[image]
        hidden = jnp.dot(
            own, ffn_first_ref[:features], preferred_element_type=jnp.float32
        ) + jnp.dot(told, ffn_first_ref[features:], preferred_element_type=jnp.float32)
        centre = jnp.mean(hidden, axis=1, keepdims=True)
        deviation = hidden - centre
        second_moment = jnp.mean(deviation * deviation, axis=1, keepdims=True)
        normed = deviation * lax.rsqrt(second_moment + 1e-05) * gain_ref[...] + bias_ref[...]
        active = 0.5 * normed * (1.0 + lax.erf(normed * math.sqrt(0.5)))
        result = own.astype(jnp.float32) + jnp.dot(
            active.astype(jnp.bfloat16), ffn_second_ref[...], preferred_element_type=jnp.float32
        )
        out_ref[image] = result.astype(jnp.bfloat16)


def shards(
    device_count,
    descriptors,
    pair_list,
    key_proj,
    value_proj,
    out_proj,
    ffn_first,
    norm_gain,
    norm_bias,
    ffn_second,
):
    img_count, points, features = descriptors.shape
    slot_count = pair_list.shape[0]
    window = WINDOW * img_count
    in_vmem = pl.BlockSpec(memory_space=pltpu.VMEM)
    in_smem = pl.BlockSpec(memory_space=pltpu.SMEM)
    in_hbm = pl.BlockSpec(memory_space=pltpu.HBM)
    keys, values, lists = pl.pallas_call(
        functools.partial(exchange_kernel, device_count),
        out_shape=(
            jax.ShapeDtypeStruct((window, points, features), jnp.bfloat16),
            jax.ShapeDtypeStruct((window, features, points), jnp.bfloat16),
            jax.ShapeDtypeStruct((REACH + 1, 8, 128), jnp.int32),
        ),
        in_specs=[in_hbm] * 4,
        out_specs=(in_hbm, in_hbm, in_vmem),
        scratch_shapes=[
            pltpu.VMEM(descriptors.shape, jnp.bfloat16),
            pltpu.VMEM(pair_list.shape[::-1], jnp.int32),
            pltpu.VMEM(key_proj.shape, jnp.bfloat16),
            pltpu.VMEM(value_proj.shape, jnp.bfloat16),
            pltpu.VMEM((window, points, features), jnp.bfloat16),
            pltpu.VMEM((window, features, points), jnp.bfloat16),
            pltpu.VMEM((4, img_count, points, features), jnp.bfloat16),
            pltpu.VMEM((5, 8, 128), jnp.int32),
            pltpu.SemaphoreType.DMA((4,)),
            pltpu.SemaphoreType.DMA((window, 2)),
            pltpu.SemaphoreType.DMA((4, CHUNKS + 1)),
            pltpu.SemaphoreType.DMA((4, CHUNKS + 1)),
        ],
        compiler_params=pltpu.CompilerParams(
            collective_id=0, has_side_effects=True, vmem_limit_bytes=VMEM_BYTES
        ),
        name="exchange",
    )(descriptors, pair_list.T, key_proj, value_proj)
    return pl.pallas_call(
        functools.partial(attend_kernel, slot_count),
        out_shape=jax.ShapeDtypeStruct(descriptors.shape, jnp.bfloat16),
        in_specs=[in_smem] + [in_hbm] * 8,
        out_specs=in_vmem,
        scratch_shapes=[
            pltpu.VMEM(keys.shape, jnp.bfloat16),
            pltpu.VMEM(values.shape, jnp.bfloat16),
            pltpu.VMEM(descriptors.shape, jnp.bfloat16),
            pltpu.VMEM(out_proj.shape, jnp.bfloat16),
            pltpu.VMEM(ffn_first.shape, jnp.bfloat16),
            pltpu.VMEM((1,) + norm_gain.shape, jnp.float32),
            pltpu.VMEM((1,) + norm_bias.shape, jnp.float32),
            pltpu.VMEM(ffn_second.shape, jnp.bfloat16),
            pltpu.VMEM((HEADS * points, features), jnp.bfloat16),
            pltpu.VMEM((8, 2 * points), jnp.float32),
            pltpu.VMEM((HEADS, features // HEADS + ONES_ROWS, points), jnp.float32),
            pltpu.SMEM((img_count, window), jnp.int32),
            pltpu.SMEM((img_count, window + 1), jnp.int32),
            pltpu.SMEM((img_count,), jnp.int32),
            pltpu.SMEM((window,), jnp.int32),
            pltpu.SemaphoreType.DMA((6,)),
            pltpu.SemaphoreType.DMA((window, 2)),
        ],
        compiler_params=pltpu.CompilerParams(vmem_limit_bytes=VMEM_BYTES),
        name="attend",
    )(
        lists,
        keys,
        values,
        descriptors,
        out_proj,
        ffn_first,
        norm_gain.reshape(1, -1),
        norm_bias.reshape(1, -1),
        ffn_second,
    )


def solution(mesh):
    in_specs = (
        P(("groups", "img"), None, None),
        P(("groups", "img"), None),
        P(),
        P(),
        P(),
        P(),
        P(),
        P(),
        P(),
    )
    out_specs = P(("groups", "img"), None, None)
    return jax.shard_map(
        functools.partial(shards, mesh.shape["img"]),
        mesh=mesh,
        in_specs=in_specs,
        out_specs=out_specs,
        check_vma=False,
    )
```

```python
import functools
import math

import jax
import jax.numpy as jnp
from jax import lax
from jax.experimental import pallas as pl
from jax.experimental.pallas import tpu as pltpu
from jax.sharding import PartitionSpec as P

HEADS = 4
REACH = 2
WINDOW = 2 * REACH + 1
CHUNKS = 8
LAG = 4
FLOW_PARTNER, FLOW_FACING, FLOW_RELAY, FLOW_SHARED = range(4)
ONES_ROWS = 16
VERY_LOW = -1e30
VMEM_BYTES = 60 * 2**20


def project(rows, key_proj, value_proj_t):
    keys = jnp.dot(rows, key_proj, preferred_element_type=jnp.float32)
    values_t = lax.dot_general(
        value_proj_t, rows, (((1,), (1,)), ((), ())), preferred_element_type=jnp.float32
    )
    return keys.astype(jnp.bfloat16), values_t.astype(jnp.bfloat16)


def exchange_kernel(
    device_count,
    own_hbm,
    pairs_hbm,
    key_proj_hbm,
    value_proj_hbm,
    keys_hbm,
    values_hbm,
    lists_ref,
    own_ref,
    pairs_ref,
    key_proj_ref,
    value_proj_ref,
    keys_ref,
    values_ref,
    land,
    land_lists,
    fetch_sems,
    store_sems,
    send_sems,
    recv_sems,
):
    img_count, points, features = own_hbm.shape
    me = lax.axis_index("img")
    chip = lax.div(me, 2)
    core = lax.rem(me, 2)
    odd = lax.rem(chip, 2)
    chip_count = device_count // 2
    partner = me + 1 - 2 * core
    facing = me + 2 * (1 - 2 * odd)
    relay_to = me + 4 * (1 - 2 * odd)
    relay_from = me - 4 * (1 - 2 * odd)
    gives_relay = (relay_to >= 0) & (relay_to < 2 * chip_count)
    gets_relay = (relay_from >= 0) & (relay_from < 2 * chip_count)
    shares_facing = odd == core
    shares_relay = (odd != core) & gets_relay
    gets_shared = (odd != core) | gets_relay

    fetches = [
        pltpu.make_async_copy(source, target, fetch_sems.at[index])
        for index, (source, target) in enumerate(
            (
                (pairs_hbm, pairs_ref),
                (own_hbm, own_ref),
                (key_proj_hbm, key_proj_ref),
                (value_proj_hbm, value_proj_ref),
            )
        )
    ]
    for fetch in fetches:
        fetch.start()
    land_lists[...] = jnp.full(land_lists.shape, -1, jnp.int32)

    barrier = pltpu.get_barrier_semaphore()

    def greet(device):
        pl.semaphore_signal(
            barrier, inc=1, device_id={"img": device}, device_id_type=pl.DeviceIdType.MESH
        )

    greet(partner)
    greet(facing)

    @pl.when(gives_relay)
    def _():
        greet(relay_to)

    @pl.when(gets_relay)
    def _():
        greet(relay_from)

    pl.semaphore_wait(
        barrier, 2 + gives_relay.astype(jnp.int32) + gets_relay.astype(jnp.int32)
    )

    pieces = CHUNKS // img_count
    rows = points // pieces

    def transfer(flow, part, source, device):
        if part == CHUNKS:
            src = land_lists.at[source]
            dst = land_lists.at[flow + 1]
        else:
            spot = (part // pieces, pl.ds((part % pieces) * rows, rows))
            src = own_hbm.at[spot] if source == 0 else land.at[(source - 1,) + spot]
            dst = land.at[(flow,) + spot]
        return pltpu.make_async_remote_copy(
            src_ref=src,
            dst_ref=dst,
            send_sem=send_sems.at[flow, part],
            recv_sem=recv_sems.at[flow, part],
            device_id={"img": device},
            device_id_type=pl.DeviceIdType.MESH,
        )

    parts = list(range(CHUNKS)) + [CHUNKS]
    for part in range(CHUNKS):
        transfer(FLOW_FACING, part, 0, facing).start()
    for part in range(CHUNKS):
        transfer(FLOW_PARTNER, part, 0, partner).start()
    fetches[0].wait()
    land_lists[0, 0 : pairs_ref.shape[0], 0 : pairs_ref.shape[1]] = pairs_ref[...]
    transfer(FLOW_FACING, CHUNKS, 0, facing).start()
    transfer(FLOW_PARTNER, CHUNKS, 0, partner).start()
    for fetch in fetches[1:]:
        fetch.wait()

    def after_facing(part):
        transfer(FLOW_FACING, part, 0, facing).wait_recv()

        @pl.when(gives_relay)
        def _():
            transfer(FLOW_RELAY, part, 1 + FLOW_FACING, relay_to).start()

        @pl.when(shares_facing)
        def _():
            transfer(FLOW_SHARED, part, 1 + FLOW_FACING, partner).start()

    def after_relay(part):
        @pl.when(gets_relay)
        def _():
            transfer(FLOW_RELAY, part, 1 + FLOW_FACING, relay_from).wait_recv()

        @pl.when(shares_relay)
        def _():
            transfer(FLOW_SHARED, part, 1 + FLOW_RELAY, partner).start()

    value_proj_t = value_proj_ref[...].T
    key_proj = key_proj_ref[...]

    def stores(slot, place, image):
        return [
            pltpu.make_async_copy(
                source.at[img_count * slot + image],
                target.at[img_count * place + image],
                store_sems.at[img_count * slot + image, index],
            )
            for index, (source, target) in enumerate(
                ((keys_ref, keys_hbm), (values_ref, values_hbm))
            )
        ]

    def project_image(slot, place, block_ref, image):
        keys, values_t = project(block_ref[image], key_proj, value_proj_t)
        keys_ref[img_count * slot + image] = keys
        values_ref[img_count * slot + image] = values_t
        for store in stores(slot, place, image):
            store.start()

    place_partner = REACH + 1 - 2 * core
    place_shared = REACH - 1 + 2 * core
    place_facing = 2 * REACH * (1 - odd)
    place_relay = 2 * REACH * odd

    def take_partner(image):
        for part in range(image * pieces, (image + 1) * pieces):
            transfer(FLOW_PARTNER, part, 0, partner).wait_recv()
        project_image(1 + FLOW_PARTNER, place_partner, land.at[FLOW_PARTNER], image)

    def take_relay(image):
        @pl.when(gets_relay)
        def _():
            project_image(1 + FLOW_RELAY, place_relay, land.at[FLOW_RELAY], image)

    def take_shared(image):
        @pl.when(gets_shared)
        def _():
            for part in range(image * pieces, (image + 1) * pieces):
                transfer(FLOW_SHARED, part, 1 + FLOW_FACING, partner).wait_recv()
            project_image(1 + FLOW_SHARED, place_shared, land.at[FLOW_SHARED], image)

    meanwhile = {}
    for image in range(img_count):
        meanwhile.setdefault(image, []).append(functools.partial(take_partner, image))
        if image + 1 < img_count:
            done = (image + 1) * pieces
            meanwhile.setdefault(done - 1, []).append(
                functools.partial(
                    project_image, 1 + FLOW_FACING, place_facing, land.at[FLOW_FACING], image
                )
            )
            meanwhile.setdefault(done - 1 + LAG, []).append(
                functools.partial(take_relay, image)
            )
            meanwhile.setdefault(done + LAG, []).append(functools.partial(take_shared, image))

    for image in range(img_count):
        project_image(0, REACH, own_ref, image)
    for step in range(CHUNKS + LAG):
        if step < CHUNKS:
            after_facing(step)
        if step >= LAG:
            after_relay(step - LAG)
        for task in meanwhile.get(step, []):
            task()
        if step == CHUNKS - 1:
            after_facing(CHUNKS)
            transfer(FLOW_PARTNER, CHUNKS, 0, partner).wait_recv()
            project_image(1 + FLOW_FACING, place_facing, land.at[FLOW_FACING], img_count - 1)
    after_relay(CHUNKS)
    take_relay(img_count - 1)
    take_shared(img_count - 1)

    @pl.when(gets_shared)
    def _():
        transfer(FLOW_SHARED, CHUNKS, 1 + FLOW_FACING, partner).wait_recv()

    for part in parts:
        transfer(FLOW_FACING, part, 0, facing).wait_send()
        transfer(FLOW_PARTNER, part, 0, partner).wait_send()

        @pl.when(gives_relay)
        def _():
            transfer(FLOW_RELAY, part, 1 + FLOW_FACING, relay_to).wait_send()

        @pl.when(shares_facing)
        def _():
            transfer(FLOW_SHARED, part, 1 + FLOW_FACING, partner).wait_send()

        @pl.when(shares_relay)
        def _():
            transfer(FLOW_SHARED, part, 1 + FLOW_RELAY, partner).wait_send()

    for image in range(img_count):
        for slot, place in (
            (0, REACH),
            (1 + FLOW_PARTNER, place_partner),
            (1 + FLOW_FACING, place_facing),
        ):
            for store in stores(slot, place, image):
                store.wait()

        @pl.when(gets_relay)
        def _():
            for store in stores(1 + FLOW_RELAY, place_relay, image):
                store.wait()

        @pl.when(gets_shared)
        def _():
            for store in stores(1 + FLOW_SHARED, place_shared, image):
                store.wait()

    behind_two = jnp.where(odd == 1, land_lists[1 + FLOW_FACING], land_lists[1 + FLOW_RELAY])
    behind_one = jnp.where(core == 1, land_lists[1 + FLOW_PARTNER], land_lists[1 + FLOW_SHARED])
    first_image = (me - REACH) * img_count
    for place, entries in enumerate((behind_two, behind_one, land_lists[0])):
        lists_ref[place] = jnp.where(entries >= 0, entries - first_image, -1)


def attend_kernel(
    slot_count,
    lists_ref,
    keys_hbm,
    values_hbm,
    own_hbm,
    out_proj_hbm,
    ffn_first_hbm,
    gain_hbm,
    bias_hbm,
    ffn_second_hbm,
    out_ref,
    keys_ref,
    values_ref,
    own_ref,
    out_proj_ref,
    ffn_first_ref,
    gain_ref,
    bias_ref,
    ffn_second_ref,
    queries,
    maxima,
    sums,
    repeats,
    sources,
    counts,
    arrived,
    fetch_sems,
    load_sems,
):
    img_count, points, features = own_ref.shape
    head_size = features // HEADS
    window = keys_ref.shape[0]
    first_own = REACH * img_count

    fetches = [
        pltpu.make_async_copy(source, target, fetch_sems.at[index])
        for index, (source, target) in enumerate(
            (
                (own_hbm, own_ref),
                (out_proj_hbm, out_proj_ref),
                (ffn_first_hbm, ffn_first_ref),
                (gain_hbm, gain_ref),
                (bias_hbm, bias_ref),
                (ffn_second_hbm, ffn_second_ref),
            )
        )
    ]

    def loads(source):
        return [
            pltpu.make_async_copy(held.at[source], to.at[source], load_sems.at[source, index])
            for index, (held, to) in enumerate(((keys_hbm, keys_ref), (values_hbm, values_ref)))
        ]

    for local in range(img_count):
        for load in loads(first_own + local):
            load.start()

    for local in range(img_count):
        for source in range(window):
            repeats[local, source] = 0

    def note(image, source):
        wanted = (image >= first_own) & (image < first_own + img_count)

        @pl.when(wanted)
        def _():
            local = image - first_own
            repeats[local, source] = repeats[local, source] + 1

    for group in range(REACH + 1):
        for slot in range(slot_count):
            first = lists_ref[group, 0, slot]
            second = lists_ref[group, 1, slot]
            if group == REACH:
                note(first, second)
            note(second, first)

    for local in range(img_count):
        held = jnp.int32(0)
        for source in range(window):
            sources[local, held] = source
            held = held + (repeats[local, source] > 0).astype(jnp.int32)
        counts[local] = held

    for source in range(window):
        is_own = first_own <= source < first_own + img_count
        arrived[source] = int(is_own)
        if not is_own:
            used = repeats[0, source]
            for local in range(1, img_count):
                used = used + repeats[local, source]

            @pl.when(used > 0)
            def _():
                for load in loads(source):
                    load.start()

    for fetch in fetches:
        fetch.start()
    for local in range(img_count):
        for load in loads(first_own + local):
            load.wait()

    head_of = lax.broadcasted_iota(jnp.int32, (features, points), 0) // head_size
    ones = jnp.ones((ONES_ROWS, points), jnp.bfloat16)

    @pl.loop(0, img_count)
    def _(image):
        own_keys = keys_ref[first_own + image].astype(jnp.float32).T * (
            1.0 / math.sqrt(head_size)
        )
        for h in range(HEADS):
            queries[:, h * points : (h + 1) * points] = jnp.where(
                head_of == h, own_keys, 0.0
            ).astype(jnp.bfloat16)
        maxima[...] = jnp.full(maxima.shape, VERY_LOW, jnp.float32)
        sums[...] = jnp.zeros(sums.shape, jnp.float32)

        @pl.loop(0, counts[image])
        def _(index):
            source = sources[image, index]

            @pl.when(arrived[source] == 0)
            def _():
                for load in loads(source):
                    load.wait()
                arrived[source] = 1

            times = repeats[image, source].astype(jnp.float32)
            keys = keys_ref[source]
            values_t = values_ref[source]
            for pair in range(HEADS // 2):
                scores = jnp.dot(
                    keys,
                    queries[:, 2 * pair * points : 2 * (pair + 1) * points],
                    preferred_element_type=jnp.float32,
                )
                held_max = maxima[pair : pair + 1]
                top = jnp.maximum(held_max, jnp.max(scores, axis=0, keepdims=True))
                weights = jnp.exp((scores - top).astype(jnp.bfloat16))
                decay = jnp.exp(held_max - top)
                maxima[pair : pair + 1] = top
                for side in range(2):
                    h = 2 * pair + side
                    with_ones = jnp.concatenate(
                        [values_t[h * head_size : (h + 1) * head_size], ones], axis=0
                    )
                    span = slice(side * points, (side + 1) * points)
                    added = jnp.dot(
                        with_ones, weights[:, span], preferred_element_type=jnp.float32
                    )
                    sums[h] = sums[h] * decay[:, span] + added * times

        @pl.when(image == 0)
        def _():
            for fetch in fetches:
                fetch.wait()

        message = jnp.concatenate(
            [sums[h, :head_size] / sums[h, head_size : head_size + 1] for h in range(HEADS)],
            axis=0,
        )
        message = message.T.astype(jnp.bfloat16)
        told = jnp.dot(message, out_proj_ref[...], preferred_element_type=jnp.float32).astype(
            jnp.bfloat16
        )
        own = own_ref[image]
        hidden = jnp.dot(
            own, ffn_first_ref[:features], preferred_element_type=jnp.float32
        ) + jnp.dot(told, ffn_first_ref[features:], preferred_element_type=jnp.float32)
        centre = jnp.mean(hidden, axis=1, keepdims=True)
        deviation = hidden - centre
        second_moment = jnp.mean(deviation * deviation, axis=1, keepdims=True)
        normed = deviation * lax.rsqrt(second_moment + 1e-05) * gain_ref[...] + bias_ref[...]
        active = 0.5 * normed * (1.0 + lax.erf(normed * math.sqrt(0.5)))
        result = own.astype(jnp.float32) + jnp.dot(
            active.astype(jnp.bfloat16), ffn_second_ref[...], preferred_element_type=jnp.float32
        )
        out_ref[image] = result.astype(jnp.bfloat16)


def shards(
    device_count,
    descriptors,
    pair_list,
    key_proj,
    value_proj,
    out_proj,
    ffn_first,
    norm_gain,
    norm_bias,
    ffn_second,
):
    img_count, points, features = descriptors.shape
    slot_count = pair_list.shape[0]
    window = WINDOW * img_count
    in_vmem = pl.BlockSpec(memory_space=pltpu.VMEM)
    in_smem = pl.BlockSpec(memory_space=pltpu.SMEM)
    in_hbm = pl.BlockSpec(memory_space=pltpu.HBM)
    keys, values, lists = pl.pallas_call(
        functools.partial(exchange_kernel, device_count),
        out_shape=(
            jax.ShapeDtypeStruct((window, points, features), jnp.bfloat16),
            jax.ShapeDtypeStruct((window, features, points), jnp.bfloat16),
            jax.ShapeDtypeStruct((REACH + 1, 8, 128), jnp.int32),
        ),
        in_specs=[in_hbm] * 4,
        out_specs=(in_hbm, in_hbm, in_vmem),
        scratch_shapes=[
            pltpu.VMEM(descriptors.shape, jnp.bfloat16),
            pltpu.VMEM(pair_list.shape[::-1], jnp.int32),
            pltpu.VMEM(key_proj.shape, jnp.bfloat16),
            pltpu.VMEM(value_proj.shape, jnp.bfloat16),
            pltpu.VMEM((window, points, features), jnp.bfloat16),
            pltpu.VMEM((window, features, points), jnp.bfloat16),
            pltpu.VMEM((4, img_count, points, features), jnp.bfloat16),
            pltpu.VMEM((5, 8, 128), jnp.int32),
            pltpu.SemaphoreType.DMA((4,)),
            pltpu.SemaphoreType.DMA((window, 2)),
            pltpu.SemaphoreType.DMA((4, CHUNKS + 1)),
            pltpu.SemaphoreType.DMA((4, CHUNKS + 1)),
        ],
        compiler_params=pltpu.CompilerParams(
            collective_id=0, has_side_effects=True, vmem_limit_bytes=VMEM_BYTES
        ),
        name="exchange",
    )(descriptors, pair_list.T, key_proj, value_proj)
    return pl.pallas_call(
        functools.partial(attend_kernel, slot_count),
        out_shape=jax.ShapeDtypeStruct(descriptors.shape, jnp.bfloat16),
        in_specs=[in_smem] + [in_hbm] * 8,
        out_specs=in_vmem,
        scratch_shapes=[
            pltpu.VMEM(keys.shape, jnp.bfloat16),
            pltpu.VMEM(values.shape, jnp.bfloat16),
            pltpu.VMEM(descriptors.shape, jnp.bfloat16),
            pltpu.VMEM(out_proj.shape, jnp.bfloat16),
            pltpu.VMEM(ffn_first.shape, jnp.bfloat16),
            pltpu.VMEM((1,) + norm_gain.shape, jnp.float32),
            pltpu.VMEM((1,) + norm_bias.shape, jnp.float32),
            pltpu.VMEM(ffn_second.shape, jnp.bfloat16),
            pltpu.VMEM((features, HEADS * points), jnp.bfloat16),
            pltpu.VMEM((8, 2 * points), jnp.float32),
            pltpu.VMEM((HEADS, features // HEADS + ONES_ROWS, points), jnp.float32),
            pltpu.SMEM((img_count, window), jnp.int32),
            pltpu.SMEM((img_count, window + 1), jnp.int32),
            pltpu.SMEM((img_count,), jnp.int32),
            pltpu.SMEM((window,), jnp.int32),
            pltpu.SemaphoreType.DMA((6,)),
            pltpu.SemaphoreType.DMA((window, 2)),
        ],
        compiler_params=pltpu.CompilerParams(vmem_limit_bytes=VMEM_BYTES),
        name="attend",
    )(
        lists,
        keys,
        values,
        descriptors,
        out_proj,
        ffn_first,
        norm_gain.reshape(1, -1),
        norm_bias.reshape(1, -1),
        ffn_second,
    )


def solution(mesh):
    in_specs = (
        P(("groups", "img"), None, None),
        P(("groups", "img"), None),
        P(),
        P(),
        P(),
        P(),
        P(),
        P(),
        P(),
    )
    out_specs = P(("groups", "img"), None, None)
    return jax.shard_map(
        functools.partial(shards, mesh.shape["img"]),
        mesh=mesh,
        in_specs=in_specs,
        out_specs=out_specs,
        check_vma=False,
    )
```

```python
import functools
import math

import jax
import jax.numpy as jnp
from jax import lax
from jax.experimental import pallas as pl
from jax.experimental.pallas import tpu as pltpu
from jax.sharding import PartitionSpec as P

HEADS = 4
REACH = 2
WINDOW = 2 * REACH + 1
CHUNKS = 8
LAG = 4
FLOW_PARTNER, FLOW_FACING, FLOW_RELAY, FLOW_SHARED = range(4)
ONES_ROWS = 16
VERY_LOW = -1e30
VMEM_BYTES = 60 * 2**20


def project(rows, key_proj, value_proj_t):
    keys = jnp.dot(rows, key_proj, preferred_element_type=jnp.float32)
    values_t = lax.dot_general(
        value_proj_t, rows, (((1,), (1,)), ((), ())), preferred_element_type=jnp.float32
    )
    return keys.astype(jnp.bfloat16), values_t.astype(jnp.bfloat16)


def fill_queries(queries, keys):
    points, features = keys.shape
    head_size = features // HEADS
    head_of = lax.broadcasted_iota(jnp.int32, (features, points), 0) // head_size
    keys_t = keys.astype(jnp.float32).T * (1.0 / math.sqrt(head_size))
    for h in range(HEADS):
        queries[:, h * points : (h + 1) * points] = jnp.where(head_of == h, keys_t, 0.0).astype(
            jnp.bfloat16
        )


def exchange_kernel(
    device_count,
    own_hbm,
    pairs_hbm,
    key_proj_hbm,
    value_proj_hbm,
    keys_hbm,
    values_hbm,
    sums_hbm,
    maxima_hbm,
    lists_ref,
    own_ref,
    pairs_ref,
    key_proj_ref,
    value_proj_ref,
    keys_ref,
    values_ref,
    land,
    land_lists,
    queries,
    sums,
    maxima,
    fetch_sems,
    store_sems,
    state_sems,
    send_sems,
    recv_sems,
):
    img_count, points, features = own_hbm.shape
    me = lax.axis_index("img")
    chip = lax.div(me, 2)
    core = lax.rem(me, 2)
    odd = lax.rem(chip, 2)
    chip_count = device_count // 2
    partner = me + 1 - 2 * core
    facing = me + 2 * (1 - 2 * odd)
    relay_to = me + 4 * (1 - 2 * odd)
    relay_from = me - 4 * (1 - 2 * odd)
    gives_relay = (relay_to >= 0) & (relay_to < 2 * chip_count)
    gets_relay = (relay_from >= 0) & (relay_from < 2 * chip_count)
    shares_facing = odd == core
    shares_relay = (odd != core) & gets_relay
    gets_shared = (odd != core) | gets_relay

    fetches = [
        pltpu.make_async_copy(source, target, fetch_sems.at[index])
        for index, (source, target) in enumerate(
            (
                (pairs_hbm, pairs_ref),
                (own_hbm, own_ref),
                (key_proj_hbm, key_proj_ref),
                (value_proj_hbm, value_proj_ref),
            )
        )
    ]
    for fetch in fetches:
        fetch.start()
    land_lists[...] = jnp.full(land_lists.shape, -1, jnp.int32)

    barrier = pltpu.get_barrier_semaphore()

    def greet(device):
        pl.semaphore_signal(
            barrier, inc=1, device_id={"img": device}, device_id_type=pl.DeviceIdType.MESH
        )

    greet(partner)
    greet(facing)

    @pl.when(gives_relay)
    def _():
        greet(relay_to)

    @pl.when(gets_relay)
    def _():
        greet(relay_from)

    pl.semaphore_wait(
        barrier, 2 + gives_relay.astype(jnp.int32) + gets_relay.astype(jnp.int32)
    )

    pieces = CHUNKS // img_count
    rows = points // pieces

    def transfer(flow, part, source, device):
        if part == CHUNKS:
            src = land_lists.at[source]
            dst = land_lists.at[flow + 1]
        else:
            spot = (part // pieces, pl.ds((part % pieces) * rows, rows))
            src = own_hbm.at[spot] if source == 0 else land.at[(source - 1,) + spot]
            dst = land.at[(flow,) + spot]
        return pltpu.make_async_remote_copy(
            src_ref=src,
            dst_ref=dst,
            send_sem=send_sems.at[flow, part],
            recv_sem=recv_sems.at[flow, part],
            device_id={"img": device},
            device_id_type=pl.DeviceIdType.MESH,
        )

    parts = list(range(CHUNKS)) + [CHUNKS]
    for part in range(CHUNKS):
        transfer(FLOW_FACING, part, 0, facing).start()
    for part in range(CHUNKS):
        transfer(FLOW_PARTNER, part, 0, partner).start()
    fetches[0].wait()
    land_lists[0, 0 : pairs_ref.shape[0], 0 : pairs_ref.shape[1]] = pairs_ref[...]
    transfer(FLOW_FACING, CHUNKS, 0, facing).start()
    transfer(FLOW_PARTNER, CHUNKS, 0, partner).start()
    for fetch in fetches[1:]:
        fetch.wait()

    def after_facing(part):
        transfer(FLOW_FACING, part, 0, facing).wait_recv()

        @pl.when(gives_relay)
        def _():
            transfer(FLOW_RELAY, part, 1 + FLOW_FACING, relay_to).start()

        @pl.when(shares_facing)
        def _():
            transfer(FLOW_SHARED, part, 1 + FLOW_FACING, partner).start()

    def after_relay(part):
        @pl.when(gets_relay)
        def _():
            transfer(FLOW_RELAY, part, 1 + FLOW_FACING, relay_from).wait_recv()

        @pl.when(shares_relay)
        def _():
            transfer(FLOW_SHARED, part, 1 + FLOW_RELAY, partner).start()

    value_proj_t = value_proj_ref[...].T
    key_proj = key_proj_ref[...]

    def stores(slot, place, image):
        return [
            pltpu.make_async_copy(
                source.at[img_count * slot + image],
                target.at[img_count * place + image],
                store_sems.at[img_count * slot + image, index],
            )
            for index, (source, target) in enumerate(
                ((keys_ref, keys_hbm), (values_ref, values_hbm))
            )
        ]

    def project_image(slot, place, block_ref, image):
        keys, values_t = project(block_ref[image], key_proj, value_proj_t)
        keys_ref[img_count * slot + image] = keys
        values_ref[img_count * slot + image] = values_t
        for store in stores(slot, place, image):
            store.start()

    place_partner = REACH + 1 - 2 * core
    place_shared = REACH - 1 + 2 * core
    place_facing = 2 * REACH * (1 - odd)
    place_relay = 2 * REACH * odd

    def take_partner(image):
        for part in range(image * pieces, (image + 1) * pieces):
            transfer(FLOW_PARTNER, part, 0, partner).wait_recv()
        project_image(1 + FLOW_PARTNER, place_partner, land.at[FLOW_PARTNER], image)

    def take_relay(image):
        @pl.when(gets_relay)
        def _():
            project_image(1 + FLOW_RELAY, place_relay, land.at[FLOW_RELAY], image)

    def take_shared(image):
        @pl.when(gets_shared)
        def _():
            for part in range(image * pieces, (image + 1) * pieces):
                transfer(FLOW_SHARED, part, 1 + FLOW_FACING, partner).wait_recv()
            project_image(1 + FLOW_SHARED, place_shared, land.at[FLOW_SHARED], image)

    meanwhile = {}
    for image in range(img_count):
        meanwhile.setdefault(image, []).append(functools.partial(take_partner, image))
        if image + 1 < img_count:
            done = (image + 1) * pieces
            meanwhile.setdefault(done - 1, []).append(
                functools.partial(
                    project_image, 1 + FLOW_FACING, place_facing, land.at[FLOW_FACING], image
                )
            )
            meanwhile.setdefault(done - 1 + LAG, []).append(
                functools.partial(take_relay, image)
            )
            meanwhile.setdefault(done + LAG, []).append(functools.partial(take_shared, image))

    for image in range(img_count):
        project_image(0, REACH, own_ref, image)
    ones = jnp.ones((ONES_ROWS, points), jnp.bfloat16)
    head_size = features // HEADS
    for image in range(img_count):
        fill_queries(queries.at[image], keys_ref[image])
    sums[...] = jnp.zeros(sums.shape, jnp.float32)
    maxima[...] = jnp.full(maxima.shape, VERY_LOW, jnp.float32)

    def times_named(one, other):
        total = jnp.zeros((1, 128), jnp.float32)
        for entry in (0, 1 + FLOW_PARTNER):
            first = land_lists[entry, 0:1, :]
            second = land_lists[entry, 1:2, :]
            named = ((first == one) & (second == other)) | ((first == other) & (second == one))
            total = total + jnp.where(named, 1.0, 0.0)
        total = jnp.sum(total, axis=1, keepdims=True)
        return jnp.broadcast_to(total, (1, 2 * points))

    def attend_near(image, slot, source, pair):
        home = me if slot == 0 else partner
        times = times_named(me * img_count + image, home * img_count + source)
        values_t = values_ref[img_count * slot + source]
        scores = jnp.dot(
            keys_ref[img_count * slot + source],
            queries[image, :, 2 * pair * points : 2 * (pair + 1) * points],
            preferred_element_type=jnp.float32,
        )
        top = jnp.max(scores, axis=0, keepdims=True)
        weights = jnp.exp((scores - top).astype(jnp.bfloat16))
        held_max = maxima[image, pair : pair + 1]
        new_max = jnp.where(times > 0.0, jnp.maximum(held_max, top), held_max)
        decay = jnp.exp(held_max - new_max)
        share = times * jnp.exp(jnp.minimum(top - new_max, 0.0))
        maxima[image, pair : pair + 1] = new_max
        for side in range(2):
            h = 2 * pair + side
            with_ones = jnp.concatenate(
                [values_t[h * head_size : (h + 1) * head_size], ones], axis=0
            )
            span = slice(side * points, (side + 1) * points)
            added = jnp.dot(with_ones, weights[:, span], preferred_element_type=jnp.float32)
            sums[image, h] = sums[image, h] * decay[:, span] + added * share[:, span]

    near = [
        functools.partial(attend_near, image, slot, source, pair)
        for slot in (0, 1 + FLOW_PARTNER)
        for image in range(img_count)
        for source in range(img_count)
        if slot != 0 or source != image
        for pair in range(HEADS // 2)
    ]
    steps = CHUNKS + LAG
    for step in range(steps):
        if step < CHUNKS:
            after_facing(step)
        if step >= LAG:
            after_relay(step - LAG)
        if step == 0:
            transfer(FLOW_PARTNER, CHUNKS, 0, partner).wait_recv()
        for task in meanwhile.get(step, []):
            task()
        for task in near[step * len(near) // steps : (step + 1) * len(near) // steps]:
            task()
        if step == CHUNKS - 1:
            after_facing(CHUNKS)
            project_image(1 + FLOW_FACING, place_facing, land.at[FLOW_FACING], img_count - 1)
    state_stores = [
        pltpu.make_async_copy(sums, sums_hbm, state_sems.at[0]),
        pltpu.make_async_copy(maxima, maxima_hbm, state_sems.at[1]),
    ]
    for store in state_stores:
        store.start()
    after_relay(CHUNKS)
    take_relay(img_count - 1)
    take_shared(img_count - 1)

    @pl.when(gets_shared)
    def _():
        transfer(FLOW_SHARED, CHUNKS, 1 + FLOW_FACING, partner).wait_recv()

    for part in parts:
        transfer(FLOW_FACING, part, 0, facing).wait_send()
        transfer(FLOW_PARTNER, part, 0, partner).wait_send()

        @pl.when(gives_relay)
        def _():
            transfer(FLOW_RELAY, part, 1 + FLOW_FACING, relay_to).wait_send()

        @pl.when(shares_facing)
        def _():
            transfer(FLOW_SHARED, part, 1 + FLOW_FACING, partner).wait_send()

        @pl.when(shares_relay)
        def _():
            transfer(FLOW_SHARED, part, 1 + FLOW_RELAY, partner).wait_send()

    for store in state_stores:
        store.wait()
    for image in range(img_count):
        for slot, place in (
            (0, REACH),
            (1 + FLOW_PARTNER, place_partner),
            (1 + FLOW_FACING, place_facing),
        ):
            for store in stores(slot, place, image):
                store.wait()

        @pl.when(gets_relay)
        def _():
            for store in stores(1 + FLOW_RELAY, place_relay, image):
                store.wait()

        @pl.when(gets_shared)
        def _():
            for store in stores(1 + FLOW_SHARED, place_shared, image):
                store.wait()

    behind_two = jnp.where(odd == 1, land_lists[1 + FLOW_FACING], land_lists[1 + FLOW_RELAY])
    behind_one = jnp.where(core == 1, land_lists[1 + FLOW_PARTNER], land_lists[1 + FLOW_SHARED])
    first_image = (me - REACH) * img_count
    for place, entries in enumerate((behind_two, behind_one, land_lists[0])):
        lists_ref[place] = jnp.where(entries >= 0, entries - first_image, -1)
    lists_ref[REACH + 1] = jnp.full(lists_ref.shape[1:], place_partner, jnp.int32)


def attend_kernel(
    slot_count,
    lists_ref,
    keys_hbm,
    values_hbm,
    sums_hbm,
    maxima_hbm,
    own_hbm,
    out_proj_hbm,
    ffn_first_hbm,
    gain_hbm,
    bias_hbm,
    ffn_second_hbm,
    out_ref,
    keys_ref,
    values_ref,
    own_ref,
    out_proj_ref,
    ffn_first_ref,
    gain_ref,
    bias_ref,
    ffn_second_ref,
    queries,
    maxima,
    sums,
    repeats,
    sources,
    counts,
    arrived,
    state_sems,
    fetch_sems,
    load_sems,
):
    img_count, points, features = own_ref.shape
    head_size = features // HEADS
    window = keys_ref.shape[0]
    first_own = REACH * img_count

    fetches = [
        pltpu.make_async_copy(source, target, fetch_sems.at[index])
        for index, (source, target) in enumerate(
            (
                (own_hbm, own_ref),
                (out_proj_hbm, out_proj_ref),
                (ffn_first_hbm, ffn_first_ref),
                (gain_hbm, gain_ref),
                (bias_hbm, bias_ref),
                (ffn_second_hbm, ffn_second_ref),
            )
        )
    ]

    def loads(source):
        return [
            pltpu.make_async_copy(held.at[source], to.at[source], load_sems.at[source, index])
            for index, (held, to) in enumerate(((keys_hbm, keys_ref), (values_hbm, values_ref)))
        ]

    for local in range(img_count):
        loads(first_own + local)[0].start()
    state_loads = [
        pltpu.make_async_copy(sums_hbm, sums, state_sems.at[0]),
        pltpu.make_async_copy(maxima_hbm, maxima, state_sems.at[1]),
    ]
    for load in state_loads:
        load.start()

    for local in range(img_count):
        for source in range(window):
            repeats[local, source] = 0

    def note(image, source):
        wanted = (image >= first_own) & (image < first_own + img_count)

        @pl.when(wanted)
        def _():
            local = image - first_own
            repeats[local, source] = repeats[local, source] + 1

    for group in range(REACH + 1):
        for slot in range(slot_count):
            first = lists_ref[group, 0, slot]
            second = lists_ref[group, 1, slot]
            if group == REACH:
                note(first, second)
            note(second, first)

    for local in range(img_count):
        for other in range(img_count):
            repeats[local, first_own + other] = 0
            repeats[local, lists_ref[REACH + 1, 0, 0] * img_count + other] = 0

    for local in range(img_count):
        held = jnp.int32(0)
        for source in range(window):
            sources[local, held] = source
            held = held + (repeats[local, source] > 0).astype(jnp.int32)
        counts[local] = held

    for source in range(window):
        arrived[source] = 0
        if not first_own <= source < first_own + img_count:
            used = repeats[0, source]
            for local in range(1, img_count):
                used = used + repeats[local, source]

            @pl.when(used > 0)
            def _():
                for load in loads(source):
                    load.start()

    for fetch in fetches:
        fetch.start()
    for local in range(img_count):
        loads(first_own + local)[0].wait()
    for load in state_loads:
        load.wait()

    ones = jnp.ones((ONES_ROWS, points), jnp.bfloat16)

    @pl.loop(0, img_count)
    def _(image):
        fill_queries(queries, keys_ref[first_own + image])

        @pl.loop(0, counts[image])
        def _(index):
            source = sources[image, index]

            @pl.when(arrived[source] == 0)
            def _():
                for load in loads(source):
                    load.wait()
                arrived[source] = 1

            times = repeats[image, source].astype(jnp.float32)
            keys = keys_ref[source]
            values_t = values_ref[source]
            for pair in range(HEADS // 2):
                scores = jnp.dot(
                    keys,
                    queries[:, 2 * pair * points : 2 * (pair + 1) * points],
                    preferred_element_type=jnp.float32,
                )
                held_max = maxima[image, pair : pair + 1]
                top = jnp.maximum(held_max, jnp.max(scores, axis=0, keepdims=True))
                weights = jnp.exp((scores - top).astype(jnp.bfloat16))
                decay = jnp.exp(held_max - top)
                maxima[image, pair : pair + 1] = top
                for side in range(2):
                    h = 2 * pair + side
                    with_ones = jnp.concatenate(
                        [values_t[h * head_size : (h + 1) * head_size], ones], axis=0
                    )
                    span = slice(side * points, (side + 1) * points)
                    added = jnp.dot(
                        with_ones, weights[:, span], preferred_element_type=jnp.float32
                    )
                    sums[image, h] = sums[image, h] * decay[:, span] + added * times

        @pl.when(image == 0)
        def _():
            for fetch in fetches:
                fetch.wait()

        message = jnp.concatenate(
            [sums[image, h, :head_size] / sums[image, h, head_size : head_size + 1] for h in range(HEADS)],
            axis=0,
        )
        message = message.T.astype(jnp.bfloat16)
        told = jnp.dot(message, out_proj_ref[...], preferred_element_type=jnp.float32).astype(
            jnp.bfloat16
        )
        own = own_ref[image]
        hidden = jnp.dot(
            own, ffn_first_ref[:features], preferred_element_type=jnp.float32
        ) + jnp.dot(told, ffn_first_ref[features:], preferred_element_type=jnp.float32)
        centre = jnp.mean(hidden, axis=1, keepdims=True)
        deviation = hidden - centre
        second_moment = jnp.mean(deviation * deviation, axis=1, keepdims=True)
        normed = deviation * lax.rsqrt(second_moment + 1e-05) * gain_ref[...] + bias_ref[...]
        active = 0.5 * normed * (1.0 + lax.erf(normed * math.sqrt(0.5)))
        result = own.astype(jnp.float32) + jnp.dot(
            active.astype(jnp.bfloat16), ffn_second_ref[...], preferred_element_type=jnp.float32
        )
        out_ref[image] = result.astype(jnp.bfloat16)


def shards(
    device_count,
    descriptors,
    pair_list,
    key_proj,
    value_proj,
    out_proj,
    ffn_first,
    norm_gain,
    norm_bias,
    ffn_second,
):
    img_count, points, features = descriptors.shape
    slot_count = pair_list.shape[0]
    window = WINDOW * img_count
    in_vmem = pl.BlockSpec(memory_space=pltpu.VMEM)
    in_smem = pl.BlockSpec(memory_space=pltpu.SMEM)
    in_hbm = pl.BlockSpec(memory_space=pltpu.HBM)
    totals_shape = (img_count, HEADS, features // HEADS + ONES_ROWS, points)
    maxima_shape = (img_count, 8, 2 * points)
    keys, values, sums, maxima, lists = pl.pallas_call(
        functools.partial(exchange_kernel, device_count),
        out_shape=(
            jax.ShapeDtypeStruct((window, points, features), jnp.bfloat16),
            jax.ShapeDtypeStruct((window, features, points), jnp.bfloat16),
            jax.ShapeDtypeStruct(totals_shape, jnp.float32),
            jax.ShapeDtypeStruct(maxima_shape, jnp.float32),
            jax.ShapeDtypeStruct((REACH + 2, 8, 128), jnp.int32),
        ),
        in_specs=[in_hbm] * 4,
        out_specs=(in_hbm, in_hbm, in_hbm, in_hbm, in_vmem),
        scratch_shapes=[
            pltpu.VMEM(descriptors.shape, jnp.bfloat16),
            pltpu.VMEM(pair_list.shape[::-1], jnp.int32),
            pltpu.VMEM(key_proj.shape, jnp.bfloat16),
            pltpu.VMEM(value_proj.shape, jnp.bfloat16),
            pltpu.VMEM((window, points, features), jnp.bfloat16),
            pltpu.VMEM((window, features, points), jnp.bfloat16),
            pltpu.VMEM((4, img_count, points, features), jnp.bfloat16),
            pltpu.VMEM((5, 8, 128), jnp.int32),
            pltpu.VMEM((img_count, features, HEADS * points), jnp.bfloat16),
            pltpu.VMEM(totals_shape, jnp.float32),
            pltpu.VMEM(maxima_shape, jnp.float32),
            pltpu.SemaphoreType.DMA((4,)),
            pltpu.SemaphoreType.DMA((window, 2)),
            pltpu.SemaphoreType.DMA((2,)),
            pltpu.SemaphoreType.DMA((4, CHUNKS + 1)),
            pltpu.SemaphoreType.DMA((4, CHUNKS + 1)),
        ],
        compiler_params=pltpu.CompilerParams(
            collective_id=0, has_side_effects=True, vmem_limit_bytes=VMEM_BYTES
        ),
        name="exchange",
    )(descriptors, pair_list.T, key_proj, value_proj)
    return pl.pallas_call(
        functools.partial(attend_kernel, slot_count),
        out_shape=jax.ShapeDtypeStruct(descriptors.shape, jnp.bfloat16),
        in_specs=[in_smem] + [in_hbm] * 10,
        out_specs=in_vmem,
        scratch_shapes=[
            pltpu.VMEM(keys.shape, jnp.bfloat16),
            pltpu.VMEM(values.shape, jnp.bfloat16),
            pltpu.VMEM(descriptors.shape, jnp.bfloat16),
            pltpu.VMEM(out_proj.shape, jnp.bfloat16),
            pltpu.VMEM(ffn_first.shape, jnp.bfloat16),
            pltpu.VMEM((1,) + norm_gain.shape, jnp.float32),
            pltpu.VMEM((1,) + norm_bias.shape, jnp.float32),
            pltpu.VMEM(ffn_second.shape, jnp.bfloat16),
            pltpu.VMEM((features, HEADS * points), jnp.bfloat16),
            pltpu.VMEM(maxima_shape, jnp.float32),
            pltpu.VMEM(totals_shape, jnp.float32),
            pltpu.SMEM((img_count, window), jnp.int32),
            pltpu.SMEM((img_count, window + 1), jnp.int32),
            pltpu.SMEM((img_count,), jnp.int32),
            pltpu.SMEM((window,), jnp.int32),
            pltpu.SemaphoreType.DMA((2,)),
            pltpu.SemaphoreType.DMA((6,)),
            pltpu.SemaphoreType.DMA((window, 2)),
        ],
        compiler_params=pltpu.CompilerParams(vmem_limit_bytes=VMEM_BYTES),
        name="attend",
    )(
        lists,
        keys,
        values,
        sums,
        maxima,
        descriptors,
        out_proj,
        ffn_first,
        norm_gain.reshape(1, -1),
        norm_bias.reshape(1, -1),
        ffn_second,
    )


def solution(mesh):
    in_specs = (
        P(("groups", "img"), None, None),
        P(("groups", "img"), None),
        P(),
        P(),
        P(),
        P(),
        P(),
        P(),
        P(),
    )
    out_specs = P(("groups", "img"), None, None)
    return jax.shard_map(
        functools.partial(shards, mesh.shape["img"]),
        mesh=mesh,
        in_specs=in_specs,
        out_specs=out_specs,
        check_vma=False,
    )
```

```python
import functools
import math

import jax
import jax.numpy as jnp
from jax import lax
from jax.experimental import pallas as pl
from jax.experimental.pallas import tpu as pltpu
from jax.sharding import PartitionSpec as P

HEADS = 4
REACH = 2
WINDOW = 2 * REACH + 1
CHUNKS = 8
LAG = 4
FLOW_PARTNER, FLOW_FACING, FLOW_RELAY, FLOW_SHARED = range(4)
ONES_ROWS = 16
VERY_LOW = -1e30
VMEM_BYTES = 60 * 2**20


def project(rows, key_proj, value_proj_t):
    keys = jnp.dot(rows, key_proj, preferred_element_type=jnp.float32)
    values_t = lax.dot_general(
        value_proj_t, rows, (((1,), (1,)), ((), ())), preferred_element_type=jnp.float32
    )
    return keys.astype(jnp.bfloat16), values_t.astype(jnp.bfloat16)


def fill_queries(queries, keys):
    points, features = keys.shape
    head_size = features // HEADS
    head_of = lax.broadcasted_iota(jnp.int32, (features, points), 0) // head_size
    keys_t = keys.astype(jnp.float32).T * (1.0 / math.sqrt(head_size))
    for h in range(HEADS):
        queries[:, h * points : (h + 1) * points] = jnp.where(head_of == h, keys_t, 0.0).astype(
            jnp.bfloat16
        )


def exchange_kernel(
    device_count,
    own_hbm,
    pairs_hbm,
    key_proj_hbm,
    value_proj_hbm,
    keys_hbm,
    values_hbm,
    sums_hbm,
    maxima_hbm,
    lists_ref,
    own_ref,
    pairs_ref,
    key_proj_ref,
    value_proj_ref,
    keys_ref,
    values_ref,
    land,
    land_lists,
    queries,
    sums,
    maxima,
    fetch_sems,
    store_sems,
    state_sems,
    send_sems,
    recv_sems,
):
    img_count, points, features = own_hbm.shape
    me = lax.axis_index("img")
    chip = lax.div(me, 2)
    core = lax.rem(me, 2)
    odd = lax.rem(chip, 2)
    chip_count = device_count // 2
    partner = me + 1 - 2 * core
    facing = me + 2 * (1 - 2 * odd)
    relay_to = me + 4 * (1 - 2 * odd)
    relay_from = me - 4 * (1 - 2 * odd)
    gives_relay = (relay_to >= 0) & (relay_to < 2 * chip_count)
    gets_relay = (relay_from >= 0) & (relay_from < 2 * chip_count)
    shares_facing = odd == core
    shares_relay = (odd != core) & gets_relay
    gets_shared = (odd != core) | gets_relay

    fetches = [
        pltpu.make_async_copy(source, target, fetch_sems.at[index])
        for index, (source, target) in enumerate(
            (
                (pairs_hbm, pairs_ref),
                (own_hbm, own_ref),
                (key_proj_hbm, key_proj_ref),
                (value_proj_hbm, value_proj_ref),
            )
        )
    ]
    for fetch in fetches:
        fetch.start()
    land_lists[...] = jnp.full(land_lists.shape, -1, jnp.int32)

    barrier = pltpu.get_barrier_semaphore()

    def greet(device):
        pl.semaphore_signal(
            barrier, inc=1, device_id={"img": device}, device_id_type=pl.DeviceIdType.MESH
        )

    greet(partner)
    greet(facing)

    @pl.when(gives_relay)
    def _():
        greet(relay_to)

    @pl.when(gets_relay)
    def _():
        greet(relay_from)

    pl.semaphore_wait(
        barrier, 2 + gives_relay.astype(jnp.int32) + gets_relay.astype(jnp.int32)
    )

    pieces = CHUNKS // img_count
    rows = points // pieces

    def transfer(flow, part, source, device):
        if part == CHUNKS:
            src = land_lists.at[source]
            dst = land_lists.at[flow + 1]
        else:
            spot = (part // pieces, pl.ds((part % pieces) * rows, rows))
            src = own_hbm.at[spot] if source == 0 else land.at[(source - 1,) + spot]
            dst = land.at[(flow,) + spot]
        return pltpu.make_async_remote_copy(
            src_ref=src,
            dst_ref=dst,
            send_sem=send_sems.at[flow, part],
            recv_sem=recv_sems.at[flow, part],
            device_id={"img": device},
            device_id_type=pl.DeviceIdType.MESH,
        )

    parts = list(range(CHUNKS)) + [CHUNKS]
    for part in range(CHUNKS):
        transfer(FLOW_FACING, part, 0, facing).start()
    for part in range(CHUNKS):
        transfer(FLOW_PARTNER, part, 0, partner).start()
    fetches[0].wait()
    land_lists[0, 0 : pairs_ref.shape[0], 0 : pairs_ref.shape[1]] = pairs_ref[...]
    transfer(FLOW_FACING, CHUNKS, 0, facing).start()
    transfer(FLOW_PARTNER, CHUNKS, 0, partner).start()
    for fetch in fetches[1:]:
        fetch.wait()

    def after_facing(part):
        transfer(FLOW_FACING, part, 0, facing).wait_recv()

        @pl.when(gives_relay)
        def _():
            transfer(FLOW_RELAY, part, 1 + FLOW_FACING, relay_to).start()

        @pl.when(shares_facing)
        def _():
            transfer(FLOW_SHARED, part, 1 + FLOW_FACING, partner).start()

    def after_relay(part):
        @pl.when(gets_relay)
        def _():
            transfer(FLOW_RELAY, part, 1 + FLOW_FACING, relay_from).wait_recv()

        @pl.when(shares_relay)
        def _():
            transfer(FLOW_SHARED, part, 1 + FLOW_RELAY, partner).start()

    value_proj_t = value_proj_ref[...].T
    key_proj = key_proj_ref[...]

    def stores(slot, place, image):
        return [
            pltpu.make_async_copy(
                source.at[img_count * slot + image],
                target.at[img_count * place + image],
                store_sems.at[img_count * slot + image, index],
            )
            for index, (source, target) in enumerate(
                ((keys_ref, keys_hbm), (values_ref, values_hbm))
            )
        ]

    def project_image(slot, place, block_ref, image):
        keys, values_t = project(block_ref[image], key_proj, value_proj_t)
        keys_ref[img_count * slot + image] = keys
        values_ref[img_count * slot + image] = values_t
        for store in stores(slot, place, image):
            store.start()

    place_partner = REACH + 1 - 2 * core
    place_shared = REACH - 1 + 2 * core
    place_facing = 2 * REACH * (1 - odd)
    place_relay = 2 * REACH * odd

    def take_partner(image):
        for part in range(image * pieces, (image + 1) * pieces):
            transfer(FLOW_PARTNER, part, 0, partner).wait_recv()
        project_image(1 + FLOW_PARTNER, place_partner, land.at[FLOW_PARTNER], image)

    def take_relay(image):
        @pl.when(gets_relay)
        def _():
            project_image(1 + FLOW_RELAY, place_relay, land.at[FLOW_RELAY], image)

    def take_shared(image):
        @pl.when(gets_shared)
        def _():
            for part in range(image * pieces, (image + 1) * pieces):
                transfer(FLOW_SHARED, part, 1 + FLOW_FACING, partner).wait_recv()
            project_image(1 + FLOW_SHARED, place_shared, land.at[FLOW_SHARED], image)

    meanwhile = {}
    for image in range(img_count):
        meanwhile.setdefault(image, []).append(functools.partial(take_partner, image))
        if image + 1 < img_count:
            done = (image + 1) * pieces
            meanwhile.setdefault(done - 1, []).append(
                functools.partial(
                    project_image, 1 + FLOW_FACING, place_facing, land.at[FLOW_FACING], image
                )
            )
            meanwhile.setdefault(done - 1 + LAG, []).append(
                functools.partial(take_relay, image)
            )
            meanwhile.setdefault(done + LAG, []).append(functools.partial(take_shared, image))

    for image in range(img_count):
        project_image(0, REACH, own_ref, image)
    ones = jnp.ones((ONES_ROWS, points), jnp.bfloat16)
    head_size = features // HEADS
    for image in range(img_count):
        fill_queries(queries.at[image], keys_ref[image])
    sums[...] = jnp.zeros(sums.shape, jnp.float32)
    maxima[...] = jnp.full(maxima.shape, VERY_LOW, jnp.float32)

    def times_named(one, other, entries):
        total = jnp.zeros((1, 128), jnp.float32)
        for entry in entries:
            first = land_lists[entry, 0:1, :]
            second = land_lists[entry, 1:2, :]
            named = ((first == one) & (second == other)) | ((first == other) & (second == one))
            total = total + jnp.where(named, 1.0, 0.0)
        total = jnp.sum(total, axis=1, keepdims=True)
        return jnp.broadcast_to(total, (1, 2 * points))

    def attend_near(image, slot, source, pair):
        home = me if slot == 0 else partner
        times = times_named(
            me * img_count + image,
            home * img_count + source,
            (0,) if slot == 0 else (0, slot),
        )
        values_t = values_ref[img_count * slot + source]
        scores = jnp.dot(
            keys_ref[img_count * slot + source],
            queries[image, :, 2 * pair * points : 2 * (pair + 1) * points],
            preferred_element_type=jnp.float32,
        )
        top = jnp.max(scores, axis=0, keepdims=True)
        weights = jnp.exp((scores - top).astype(jnp.bfloat16))
        held_max = maxima[image, pair : pair + 1]
        new_max = jnp.where(times > 0.0, jnp.maximum(held_max, top), held_max)
        decay = jnp.exp(held_max - new_max)
        share = times * jnp.exp(jnp.minimum(top - new_max, 0.0))
        maxima[image, pair : pair + 1] = new_max
        for side in range(2):
            h = 2 * pair + side
            with_ones = jnp.concatenate(
                [values_t[h * head_size : (h + 1) * head_size], ones], axis=0
            )
            span = slice(side * points, (side + 1) * points)
            added = jnp.dot(with_ones, weights[:, span], preferred_element_type=jnp.float32)
            sums[image, h] = sums[image, h] * decay[:, span] + added * share[:, span]

    near = [
        functools.partial(attend_near, image, slot, source, pair)
        for slot in (0, 1 + FLOW_PARTNER)
        for image in range(img_count)
        for source in range(img_count)
        if slot != 0 or source != image
        for pair in range(HEADS // 2)
    ]
    steps = CHUNKS + LAG
    for task in near[: len(near) // steps]:
        task()
    for step in range(steps):
        if step < CHUNKS:
            after_facing(step)
        if step >= LAG:
            after_relay(step - LAG)
        if step == 0:
            transfer(FLOW_PARTNER, CHUNKS, 0, partner).wait_recv()
        for task in meanwhile.get(step, []):
            task()
        for task in near[(step + 1) * len(near) // steps : (step + 2) * len(near) // steps]:
            task()
        if step == CHUNKS - 1:
            after_facing(CHUNKS)
            project_image(1 + FLOW_FACING, place_facing, land.at[FLOW_FACING], img_count - 1)
    state_stores = [
        pltpu.make_async_copy(sums, sums_hbm, state_sems.at[0]),
        pltpu.make_async_copy(maxima, maxima_hbm, state_sems.at[1]),
    ]
    for store in state_stores:
        store.start()
    after_relay(CHUNKS)
    take_relay(img_count - 1)
    take_shared(img_count - 1)

    @pl.when(gets_shared)
    def _():
        transfer(FLOW_SHARED, CHUNKS, 1 + FLOW_FACING, partner).wait_recv()

    for part in parts:
        transfer(FLOW_FACING, part, 0, facing).wait_send()
        transfer(FLOW_PARTNER, part, 0, partner).wait_send()

        @pl.when(gives_relay)
        def _():
            transfer(FLOW_RELAY, part, 1 + FLOW_FACING, relay_to).wait_send()

        @pl.when(shares_facing)
        def _():
            transfer(FLOW_SHARED, part, 1 + FLOW_FACING, partner).wait_send()

        @pl.when(shares_relay)
        def _():
            transfer(FLOW_SHARED, part, 1 + FLOW_RELAY, partner).wait_send()

    for store in state_stores:
        store.wait()
    for image in range(img_count):
        for slot, place in (
            (0, REACH),
            (1 + FLOW_PARTNER, place_partner),
            (1 + FLOW_FACING, place_facing),
        ):
            for store in stores(slot, place, image):
                store.wait()

        @pl.when(gets_relay)
        def _():
            for store in stores(1 + FLOW_RELAY, place_relay, image):
                store.wait()

        @pl.when(gets_shared)
        def _():
            for store in stores(1 + FLOW_SHARED, place_shared, image):
                store.wait()

    behind_two = jnp.where(odd == 1, land_lists[1 + FLOW_FACING], land_lists[1 + FLOW_RELAY])
    behind_one = jnp.where(core == 1, land_lists[1 + FLOW_PARTNER], land_lists[1 + FLOW_SHARED])
    first_image = (me - REACH) * img_count
    for place, entries in enumerate((behind_two, behind_one, land_lists[0])):
        used_entries = entries[: lists_ref.shape[1]]
        lists_ref[place] = jnp.where(used_entries >= 0, used_entries - first_image, -1)
    lists_ref[REACH + 1] = jnp.full(lists_ref.shape[1:], place_partner, jnp.int32)


def attend_kernel(
    slot_count,
    lists_ref,
    keys_hbm,
    values_hbm,
    sums_hbm,
    maxima_hbm,
    own_hbm,
    out_proj_hbm,
    ffn_first_hbm,
    gain_hbm,
    bias_hbm,
    ffn_second_hbm,
    out_ref,
    keys_ref,
    values_ref,
    own_ref,
    out_proj_ref,
    ffn_first_ref,
    gain_ref,
    bias_ref,
    ffn_second_ref,
    queries,
    maxima,
    sums,
    repeats,
    sources,
    counts,
    arrived,
    state_sems,
    fetch_sems,
    load_sems,
):
    img_count, points, features = own_ref.shape
    head_size = features // HEADS
    window = keys_ref.shape[0]
    first_own = REACH * img_count

    fetches = [
        pltpu.make_async_copy(source, target, fetch_sems.at[index])
        for index, (source, target) in enumerate(
            (
                (own_hbm, own_ref),
                (out_proj_hbm, out_proj_ref),
                (ffn_first_hbm, ffn_first_ref),
                (gain_hbm, gain_ref),
                (bias_hbm, bias_ref),
                (ffn_second_hbm, ffn_second_ref),
            )
        )
    ]

    def loads(source):
        return [
            pltpu.make_async_copy(held.at[source], to.at[source], load_sems.at[source, index])
            for index, (held, to) in enumerate(((keys_hbm, keys_ref), (values_hbm, values_ref)))
        ]

    for local in range(img_count):
        loads(first_own + local)[0].start()
    state_loads = [
        pltpu.make_async_copy(sums_hbm, sums, state_sems.at[0]),
        pltpu.make_async_copy(maxima_hbm, maxima, state_sems.at[1]),
    ]
    for load in state_loads:
        load.start()

    for local in range(img_count):
        for source in range(window):
            repeats[local, source] = 0

    def note(image, source):
        wanted = (image >= first_own) & (image < first_own + img_count)

        @pl.when(wanted)
        def _():
            local = image - first_own
            repeats[local, source] = repeats[local, source] + 1

    for group in range(REACH + 1):
        for slot in range(slot_count):
            first = lists_ref[group, 0, slot]
            second = lists_ref[group, 1, slot]
            if group == REACH:
                note(first, second)
            note(second, first)

    for local in range(img_count):
        for other in range(img_count):
            repeats[local, first_own + other] = 0
            repeats[local, lists_ref[REACH + 1, 0, 0] * img_count + other] = 0

    for local in range(img_count):
        held = jnp.int32(0)
        for source in range(window):
            sources[local, held] = source
            held = held + (repeats[local, source] > 0).astype(jnp.int32)
        counts[local] = held

    for source in range(window):
        arrived[source] = 0
        if not first_own <= source < first_own + img_count:
            used = repeats[0, source]
            for local in range(1, img_count):
                used = used + repeats[local, source]

            @pl.when(used > 0)
            def _():
                for load in loads(source):
                    load.start()

    for fetch in fetches:
        fetch.start()
    for local in range(img_count):
        loads(first_own + local)[0].wait()

    ones = jnp.ones((ONES_ROWS, points), jnp.bfloat16)

    @pl.loop(0, img_count)
    def _(image):
        fill_queries(queries, keys_ref[first_own + image])

        @pl.when(image == 0)
        def _():
            for load in state_loads:
                load.wait()

        @pl.loop(0, counts[image])
        def _(index):
            source = sources[image, index]

            @pl.when(arrived[source] == 0)
            def _():
                for load in loads(source):
                    load.wait()
                arrived[source] = 1

            times = repeats[image, source].astype(jnp.float32)
            keys = keys_ref[source]
            values_t = values_ref[source]
            all_scores = [
                jnp.dot(
                    keys,
                    queries[:, 2 * pair * points : 2 * (pair + 1) * points],
                    preferred_element_type=jnp.float32,
                )
                for pair in range(HEADS // 2)
            ]
            for pair, scores in enumerate(all_scores):
                held_max = maxima[image, pair : pair + 1]
                top = jnp.maximum(held_max, jnp.max(scores, axis=0, keepdims=True))
                weights = jnp.exp((scores - top).astype(jnp.bfloat16))
                decay = jnp.exp(held_max - top)
                maxima[image, pair : pair + 1] = top
                for side in range(2):
                    h = 2 * pair + side
                    with_ones = jnp.concatenate(
                        [values_t[h * head_size : (h + 1) * head_size], ones], axis=0
                    )
                    span = slice(side * points, (side + 1) * points)
                    added = jnp.dot(
                        with_ones, weights[:, span], preferred_element_type=jnp.float32
                    )
                    sums[image, h] = sums[image, h] * decay[:, span] + added * times

        @pl.when(image == 0)
        def _():
            for fetch in fetches:
                fetch.wait()

        message = jnp.concatenate(
            [sums[image, h, :head_size] / sums[image, h, head_size : head_size + 1] for h in range(HEADS)],
            axis=0,
        )
        message = message.T.astype(jnp.bfloat16)
        told = jnp.dot(message, out_proj_ref[...], preferred_element_type=jnp.float32).astype(
            jnp.bfloat16
        )
        own = own_ref[image]
        hidden = jnp.dot(
            own, ffn_first_ref[:features], preferred_element_type=jnp.float32
        ) + jnp.dot(told, ffn_first_ref[features:], preferred_element_type=jnp.float32)
        centre = jnp.mean(hidden, axis=1, keepdims=True)
        deviation = hidden - centre
        second_moment = jnp.mean(deviation * deviation, axis=1, keepdims=True)
        normed = deviation * lax.rsqrt(second_moment + 1e-05) * gain_ref[...] + bias_ref[...]
        active = 0.5 * normed * (1.0 + lax.erf(normed * math.sqrt(0.5)))
        result = own.astype(jnp.float32) + jnp.dot(
            active.astype(jnp.bfloat16), ffn_second_ref[...], preferred_element_type=jnp.float32
        )
        out_ref[image] = result.astype(jnp.bfloat16)


def shards(
    device_count,
    descriptors,
    pair_list,
    key_proj,
    value_proj,
    out_proj,
    ffn_first,
    norm_gain,
    norm_bias,
    ffn_second,
):
    img_count, points, features = descriptors.shape
    slot_count = pair_list.shape[0]
    window = WINDOW * img_count
    in_vmem = pl.BlockSpec(memory_space=pltpu.VMEM)
    in_smem = pl.BlockSpec(memory_space=pltpu.SMEM)
    in_hbm = pl.BlockSpec(memory_space=pltpu.HBM)
    totals_shape = (img_count, HEADS, features // HEADS + ONES_ROWS, points)
    maxima_shape = (img_count, 8, 2 * points)
    keys, values, sums, maxima, lists = pl.pallas_call(
        functools.partial(exchange_kernel, device_count),
        out_shape=(
            jax.ShapeDtypeStruct((window, points, features), jnp.bfloat16),
            jax.ShapeDtypeStruct((window, features, points), jnp.bfloat16),
            jax.ShapeDtypeStruct(totals_shape, jnp.float32),
            jax.ShapeDtypeStruct(maxima_shape, jnp.float32),
            jax.ShapeDtypeStruct((REACH + 2, 2, 128), jnp.int32),
        ),
        in_specs=[in_hbm] * 4,
        out_specs=(in_hbm, in_hbm, in_hbm, in_hbm, in_vmem),
        scratch_shapes=[
            pltpu.VMEM(descriptors.shape, jnp.bfloat16),
            pltpu.VMEM(pair_list.shape[::-1], jnp.int32),
            pltpu.VMEM(key_proj.shape, jnp.bfloat16),
            pltpu.VMEM(value_proj.shape, jnp.bfloat16),
            pltpu.VMEM((window, points, features), jnp.bfloat16),
            pltpu.VMEM((window, features, points), jnp.bfloat16),
            pltpu.VMEM((4, img_count, points, features), jnp.bfloat16),
            pltpu.VMEM((5, 8, 128), jnp.int32),
            pltpu.VMEM((img_count, features, HEADS * points), jnp.bfloat16),
            pltpu.VMEM(totals_shape, jnp.float32),
            pltpu.VMEM(maxima_shape, jnp.float32),
            pltpu.SemaphoreType.DMA((4,)),
            pltpu.SemaphoreType.DMA((window, 2)),
            pltpu.SemaphoreType.DMA((2,)),
            pltpu.SemaphoreType.DMA((4, CHUNKS + 1)),
            pltpu.SemaphoreType.DMA((4, CHUNKS + 1)),
        ],
        compiler_params=pltpu.CompilerParams(
            collective_id=0, has_side_effects=True, vmem_limit_bytes=VMEM_BYTES
        ),
        name="exchange",
    )(descriptors, pair_list.T, key_proj, value_proj)
    return pl.pallas_call(
        functools.partial(attend_kernel, slot_count),
        out_shape=jax.ShapeDtypeStruct(descriptors.shape, jnp.bfloat16),
        in_specs=[in_smem] + [in_hbm] * 10,
        out_specs=in_vmem,
        scratch_shapes=[
            pltpu.VMEM(keys.shape, jnp.bfloat16),
            pltpu.VMEM(values.shape, jnp.bfloat16),
            pltpu.VMEM(descriptors.shape, jnp.bfloat16),
            pltpu.VMEM(out_proj.shape, jnp.bfloat16),
            pltpu.VMEM(ffn_first.shape, jnp.bfloat16),
            pltpu.VMEM((1,) + norm_gain.shape, jnp.float32),
            pltpu.VMEM((1,) + norm_bias.shape, jnp.float32),
            pltpu.VMEM(ffn_second.shape, jnp.bfloat16),
            pltpu.VMEM((features, HEADS * points), jnp.bfloat16),
            pltpu.VMEM(maxima_shape, jnp.float32),
            pltpu.VMEM(totals_shape, jnp.float32),
            pltpu.SMEM((img_count, window), jnp.int32),
            pltpu.SMEM((img_count, window + 1), jnp.int32),
            pltpu.SMEM((img_count,), jnp.int32),
            pltpu.SMEM((window,), jnp.int32),
            pltpu.SemaphoreType.DMA((2,)),
            pltpu.SemaphoreType.DMA((6,)),
            pltpu.SemaphoreType.DMA((window, 2)),
        ],
        compiler_params=pltpu.CompilerParams(vmem_limit_bytes=VMEM_BYTES),
        name="attend",
    )(
        lists,
        keys,
        values,
        sums,
        maxima,
        descriptors,
        out_proj,
        ffn_first,
        norm_gain.reshape(1, -1),
        norm_bias.reshape(1, -1),
        ffn_second,
    )


def solution(mesh):
    in_specs = (
        P(("groups", "img"), None, None),
        P(("groups", "img"), None),
        P(),
        P(),
        P(),
        P(),
        P(),
        P(),
        P(),
    )
    out_specs = P(("groups", "img"), None, None)
    return jax.shard_map(
        functools.partial(shards, mesh.shape["img"]),
        mesh=mesh,
        in_specs=in_specs,
        out_specs=out_specs,
        check_vma=False,
    )
```

```python
import functools
import math

import jax
import jax.numpy as jnp
from jax import lax
from jax.experimental import pallas as pl
from jax.experimental.pallas import tpu as pltpu
from jax.sharding import PartitionSpec as P

HEADS = 4
REACH = 2
WINDOW = 2 * REACH + 1
CHUNKS = 8
LAG = 4
FLOW_PARTNER, FLOW_FACING, FLOW_RELAY, FLOW_SHARED = range(4)
ONES_ROWS = 16
VERY_LOW = -1e30
VMEM_BYTES = 60 * 2**20


def project(rows, key_proj, value_proj_t):
    keys = jnp.dot(rows, key_proj, preferred_element_type=jnp.float32)
    values_t = lax.dot_general(
        value_proj_t, rows, (((1,), (1,)), ((), ())), preferred_element_type=jnp.float32
    )
    return keys.astype(jnp.bfloat16), values_t.astype(jnp.bfloat16)


def fill_queries(queries, keys):
    points, features = keys.shape
    head_size = features // HEADS
    head_of = lax.broadcasted_iota(jnp.int32, (features, points), 0) // head_size
    keys_t = keys.astype(jnp.float32).T * (1.0 / math.sqrt(head_size))
    for h in range(HEADS):
        queries[:, h * points : (h + 1) * points] = jnp.where(head_of == h, keys_t, 0.0).astype(
            jnp.bfloat16
        )


def exchange_kernel(
    device_count,
    own_hbm,
    pairs_hbm,
    key_proj_hbm,
    value_proj_hbm,
    keys_hbm,
    values_hbm,
    sums_hbm,
    maxima_hbm,
    lists_ref,
    own_ref,
    pairs_ref,
    key_proj_ref,
    value_proj_ref,
    keys_ref,
    values_ref,
    land,
    land_lists,
    queries,
    sums,
    maxima,
    fetch_sems,
    store_sems,
    state_sems,
    send_sems,
    recv_sems,
):
    img_count, points, features = own_hbm.shape
    me = lax.axis_index("img")
    chip = lax.div(me, 2)
    core = lax.rem(me, 2)
    odd = lax.rem(chip, 2)
    chip_count = device_count // 2
    partner = me + 1 - 2 * core
    facing = me + 2 * (1 - 2 * odd)
    relay_to = me + 4 * (1 - 2 * odd)
    relay_from = me - 4 * (1 - 2 * odd)
    gives_relay = (relay_to >= 0) & (relay_to < 2 * chip_count)
    gets_relay = (relay_from >= 0) & (relay_from < 2 * chip_count)
    shares_facing = odd == core
    shares_relay = (odd != core) & gets_relay
    gets_shared = (odd != core) | gets_relay

    fetches = [
        pltpu.make_async_copy(source, target, fetch_sems.at[index])
        for index, (source, target) in enumerate(
            (
                (pairs_hbm, pairs_ref),
                (own_hbm, own_ref),
                (key_proj_hbm, key_proj_ref),
                (value_proj_hbm, value_proj_ref),
            )
        )
    ]
    for fetch in fetches:
        fetch.start()
    land_lists[...] = jnp.full(land_lists.shape, -1, jnp.int32)

    barrier = pltpu.get_barrier_semaphore()

    def greet(device):
        pl.semaphore_signal(
            barrier, inc=1, device_id={"img": device}, device_id_type=pl.DeviceIdType.MESH
        )

    greet(partner)
    greet(facing)

    @pl.when(gives_relay)
    def _():
        greet(relay_to)

    @pl.when(gets_relay)
    def _():
        greet(relay_from)

    pl.semaphore_wait(
        barrier, 2 + gives_relay.astype(jnp.int32) + gets_relay.astype(jnp.int32)
    )

    pieces = CHUNKS // img_count
    rows = points // pieces

    def transfer(flow, part, source, device):
        if part == CHUNKS:
            src = land_lists.at[source]
            dst = land_lists.at[flow + 1]
        else:
            spot = (part // pieces, pl.ds((part % pieces) * rows, rows))
            src = own_hbm.at[spot] if source == 0 else land.at[(source - 1,) + spot]
            dst = land.at[(flow,) + spot]
        return pltpu.make_async_remote_copy(
            src_ref=src,
            dst_ref=dst,
            send_sem=send_sems.at[flow, part],
            recv_sem=recv_sems.at[flow, part],
            device_id={"img": device},
            device_id_type=pl.DeviceIdType.MESH,
        )

    parts = list(range(CHUNKS)) + [CHUNKS]
    for part in range(CHUNKS):
        transfer(FLOW_FACING, part, 0, facing).start()
    for part in range(CHUNKS):
        transfer(FLOW_PARTNER, part, 0, partner).start()
    fetches[0].wait()
    land_lists[0, 0 : pairs_ref.shape[0], 0 : pairs_ref.shape[1]] = pairs_ref[...]
    transfer(FLOW_FACING, CHUNKS, 0, facing).start()
    transfer(FLOW_PARTNER, CHUNKS, 0, partner).start()
    for fetch in fetches[1:]:
        fetch.wait()

    def after_facing(part):
        transfer(FLOW_FACING, part, 0, facing).wait_recv()

        @pl.when(gives_relay)
        def _():
            transfer(FLOW_RELAY, part, 1 + FLOW_FACING, relay_to).start()

        @pl.when(shares_facing)
        def _():
            transfer(FLOW_SHARED, part, 1 + FLOW_FACING, partner).start()

    def after_relay(part):
        @pl.when(gets_relay)
        def _():
            transfer(FLOW_RELAY, part, 1 + FLOW_FACING, relay_from).wait_recv()

        @pl.when(shares_relay)
        def _():
            transfer(FLOW_SHARED, part, 1 + FLOW_RELAY, partner).start()

    value_proj_t = value_proj_ref[...].T
    key_proj = key_proj_ref[...]

    def stores(slot, place, image):
        return [
            pltpu.make_async_copy(
                source.at[img_count * slot + image],
                target.at[img_count * place + image],
                store_sems.at[img_count * slot + image, index],
            )
            for index, (source, target) in enumerate(
                ((keys_ref, keys_hbm), (values_ref, values_hbm))
            )
        ]

    def project_image(slot, place, block_ref, image):
        keys, values_t = project(block_ref[image], key_proj, value_proj_t)
        keys_ref[img_count * slot + image] = keys
        values_ref[img_count * slot + image] = values_t
        for store in stores(slot, place, image):
            store.start()

    place_partner = REACH + 1 - 2 * core
    place_shared = REACH - 1 + 2 * core
    place_facing = 2 * REACH * (1 - odd)
    place_relay = 2 * REACH * odd

    def take_partner(image):
        for part in range(image * pieces, (image + 1) * pieces):
            transfer(FLOW_PARTNER, part, 0, partner).wait_recv()
        project_image(1 + FLOW_PARTNER, place_partner, land.at[FLOW_PARTNER], image)

    def take_relay(image):
        @pl.when(gets_relay)
        def _():
            project_image(1 + FLOW_RELAY, place_relay, land.at[FLOW_RELAY], image)

    def take_shared(image):
        @pl.when(gets_shared)
        def _():
            for part in range(image * pieces, (image + 1) * pieces):
                transfer(FLOW_SHARED, part, 1 + FLOW_FACING, partner).wait_recv()
            project_image(1 + FLOW_SHARED, place_shared, land.at[FLOW_SHARED], image)

    meanwhile = {}
    for image in range(img_count):
        meanwhile.setdefault(image, []).append(functools.partial(take_partner, image))
        if image + 1 < img_count:
            done = (image + 1) * pieces
            meanwhile.setdefault(done - 1, []).append(
                functools.partial(
                    project_image, 1 + FLOW_FACING, place_facing, land.at[FLOW_FACING], image
                )
            )
            meanwhile.setdefault(done - 1 + LAG, []).append(
                functools.partial(take_relay, image)
            )
            meanwhile.setdefault(done + LAG, []).append(functools.partial(take_shared, image))

    for image in range(img_count):
        project_image(0, REACH, own_ref, image)
    ones = jnp.ones((ONES_ROWS, points), jnp.bfloat16)
    head_size = features // HEADS
    for image in range(img_count):
        fill_queries(queries.at[image], keys_ref[image])
    sums[...] = jnp.zeros(sums.shape, jnp.float32)
    maxima[...] = jnp.full(maxima.shape, VERY_LOW, jnp.float32)

    def times_named(one, other, entries):
        total = jnp.zeros((1, 128), jnp.float32)
        for entry in entries:
            first = land_lists[entry, 0:1, :]
            second = land_lists[entry, 1:2, :]
            named = ((first == one) & (second == other)) | ((first == other) & (second == one))
            total = total + jnp.where(named, 1.0, 0.0)
        total = jnp.sum(total, axis=1, keepdims=True)
        return jnp.broadcast_to(total, (1, 2 * points))

    def near_scores(image, slot, source, pair):
        return jnp.dot(
            keys_ref[img_count * slot + source],
            queries[image, :, 2 * pair * points : 2 * (pair + 1) * points],
            preferred_element_type=jnp.float32,
        )

    def attend_near(scores, image, slot, source, pair):
        home = me if slot == 0 else partner
        times = times_named(
            me * img_count + image,
            home * img_count + source,
            (0,) if slot == 0 else (0, slot),
        )
        values_t = values_ref[img_count * slot + source]
        top = jnp.max(scores, axis=0, keepdims=True)
        weights = jnp.exp((scores - top).astype(jnp.bfloat16))
        held_max = maxima[image, pair : pair + 1]
        new_max = jnp.where(times > 0.0, jnp.maximum(held_max, top), held_max)
        decay = jnp.exp(held_max - new_max)
        share = times * jnp.exp(jnp.minimum(top - new_max, 0.0))
        maxima[image, pair : pair + 1] = new_max
        for side in range(2):
            h = 2 * pair + side
            with_ones = jnp.concatenate(
                [values_t[h * head_size : (h + 1) * head_size], ones], axis=0
            )
            span = slice(side * points, (side + 1) * points)
            added = jnp.dot(with_ones, weights[:, span], preferred_element_type=jnp.float32)
            sums[image, h] = sums[image, h] * decay[:, span] + added * share[:, span]

    near = [
        (image, slot, source, pair)
        for slot in (0, 1 + FLOW_PARTNER)
        for image in range(img_count)
        for source in range(img_count)
        if slot != 0 or source != image
        for pair in range(HEADS // 2)
    ]
    steps = CHUNKS + LAG
    ahead = near_scores(*near[0])

    def run_near(low, high):
        nonlocal ahead
        for index in range(low, min(high, len(near))):
            scores = ahead
            if index + 1 < len(near):
                ahead = near_scores(*near[index + 1])
            attend_near(scores, *near[index])

    run_near(0, len(near) // steps)
    for step in range(steps):
        if step < CHUNKS:
            after_facing(step)
        if step >= LAG:
            after_relay(step - LAG)
        if step == 0:
            transfer(FLOW_PARTNER, CHUNKS, 0, partner).wait_recv()
        for task in meanwhile.get(step, []):
            task()
        run_near((step + 1) * len(near) // steps, (step + 2) * len(near) // steps)
        if step == CHUNKS - 1:
            after_facing(CHUNKS)
            project_image(1 + FLOW_FACING, place_facing, land.at[FLOW_FACING], img_count - 1)
    state_stores = [
        pltpu.make_async_copy(sums, sums_hbm, state_sems.at[0]),
        pltpu.make_async_copy(maxima, maxima_hbm, state_sems.at[1]),
    ]
    for store in state_stores:
        store.start()
    after_relay(CHUNKS)
    take_relay(img_count - 1)
    take_shared(img_count - 1)

    @pl.when(gets_shared)
    def _():
        transfer(FLOW_SHARED, CHUNKS, 1 + FLOW_FACING, partner).wait_recv()

    for part in parts:
        transfer(FLOW_FACING, part, 0, facing).wait_send()
        transfer(FLOW_PARTNER, part, 0, partner).wait_send()

        @pl.when(gives_relay)
        def _():
            transfer(FLOW_RELAY, part, 1 + FLOW_FACING, relay_to).wait_send()

        @pl.when(shares_facing)
        def _():
            transfer(FLOW_SHARED, part, 1 + FLOW_FACING, partner).wait_send()

        @pl.when(shares_relay)
        def _():
            transfer(FLOW_SHARED, part, 1 + FLOW_RELAY, partner).wait_send()

    for store in state_stores:
        store.wait()
    for image in range(img_count):
        for slot, place in (
            (0, REACH),
            (1 + FLOW_PARTNER, place_partner),
            (1 + FLOW_FACING, place_facing),
        ):
            for store in stores(slot, place, image):
                store.wait()

        @pl.when(gets_relay)
        def _():
            for store in stores(1 + FLOW_RELAY, place_relay, image):
                store.wait()

        @pl.when(gets_shared)
        def _():
            for store in stores(1 + FLOW_SHARED, place_shared, image):
                store.wait()

    behind_two = jnp.where(odd == 1, land_lists[1 + FLOW_FACING], land_lists[1 + FLOW_RELAY])
    behind_one = jnp.where(core == 1, land_lists[1 + FLOW_PARTNER], land_lists[1 + FLOW_SHARED])
    first_image = (me - REACH) * img_count
    for place, entries in enumerate((behind_two, behind_one, land_lists[0])):
        used_entries = entries[: lists_ref.shape[1]]
        lists_ref[place] = jnp.where(used_entries >= 0, used_entries - first_image, -1)
    lists_ref[REACH + 1] = jnp.full(lists_ref.shape[1:], place_partner, jnp.int32)


def attend_kernel(
    slot_count,
    lists_ref,
    keys_hbm,
    values_hbm,
    sums_hbm,
    maxima_hbm,
    own_hbm,
    out_proj_hbm,
    ffn_first_hbm,
    gain_hbm,
    bias_hbm,
    ffn_second_hbm,
    out_ref,
    keys_ref,
    values_ref,
    own_ref,
    out_proj_ref,
    ffn_first_ref,
    gain_ref,
    bias_ref,
    ffn_second_ref,
    queries,
    maxima,
    sums,
    repeats,
    sources,
    counts,
    arrived,
    state_sems,
    fetch_sems,
    load_sems,
):
    img_count, points, features = own_ref.shape
    head_size = features // HEADS
    window = keys_ref.shape[0]
    first_own = REACH * img_count

    fetches = [
        pltpu.make_async_copy(source, target, fetch_sems.at[index])
        for index, (source, target) in enumerate(
            (
                (own_hbm, own_ref),
                (out_proj_hbm, out_proj_ref),
                (ffn_first_hbm, ffn_first_ref),
                (gain_hbm, gain_ref),
                (bias_hbm, bias_ref),
                (ffn_second_hbm, ffn_second_ref),
            )
        )
    ]

    def loads(source):
        return [
            pltpu.make_async_copy(held.at[source], to.at[source], load_sems.at[source, index])
            for index, (held, to) in enumerate(((keys_hbm, keys_ref), (values_hbm, values_ref)))
        ]

    for local in range(img_count):
        loads(first_own + local)[0].start()
    state_loads = [
        pltpu.make_async_copy(sums_hbm, sums, state_sems.at[0]),
        pltpu.make_async_copy(maxima_hbm, maxima, state_sems.at[1]),
    ]
    for load in state_loads:
        load.start()

    for local in range(img_count):
        for source in range(window):
            repeats[local, source] = 0

    def note(image, source):
        wanted = (image >= first_own) & (image < first_own + img_count)

        @pl.when(wanted)
        def _():
            local = image - first_own
            repeats[local, source] = repeats[local, source] + 1

    for group in range(REACH + 1):
        for slot in range(slot_count):
            first = lists_ref[group, 0, slot]
            second = lists_ref[group, 1, slot]
            if group == REACH:
                note(first, second)
            note(second, first)

    for local in range(img_count):
        for other in range(img_count):
            repeats[local, first_own + other] = 0
            repeats[local, lists_ref[REACH + 1, 0, 0] * img_count + other] = 0

    for local in range(img_count):
        held = jnp.int32(0)
        for source in range(window):
            sources[local, held] = source
            held = held + (repeats[local, source] > 0).astype(jnp.int32)
        counts[local] = held

    for source in range(window):
        arrived[source] = 0
        if not first_own <= source < first_own + img_count:
            used = repeats[0, source]
            for local in range(1, img_count):
                used = used + repeats[local, source]

            @pl.when(used > 0)
            def _():
                for load in loads(source):
                    load.start()

    for fetch in fetches:
        fetch.start()
    for local in range(img_count):
        loads(first_own + local)[0].wait()

    ones = jnp.ones((ONES_ROWS, points), jnp.bfloat16)

    for image in range(img_count):
        fill_queries(queries.at[image], keys_ref[first_own + image])
    for load in state_loads:
        load.wait()

    @pl.loop(0, img_count)
    def _(image):
        @pl.loop(0, counts[image])
        def _(index):
            source = sources[image, index]

            @pl.when(arrived[source] == 0)
            def _():
                for load in loads(source):
                    load.wait()
                arrived[source] = 1

            times = repeats[image, source].astype(jnp.float32)
            keys = keys_ref[source]
            values_t = values_ref[source]
            all_scores = [
                jnp.dot(
                    keys,
                    queries[image, :, 2 * pair * points : 2 * (pair + 1) * points],
                    preferred_element_type=jnp.float32,
                )
                for pair in range(HEADS // 2)
            ]
            for pair, scores in enumerate(all_scores):
                held_max = maxima[image, pair : pair + 1]
                top = jnp.maximum(held_max, jnp.max(scores, axis=0, keepdims=True))
                weights = jnp.exp((scores - top).astype(jnp.bfloat16))
                decay = jnp.exp(held_max - top)
                maxima[image, pair : pair + 1] = top
                for side in range(2):
                    h = 2 * pair + side
                    with_ones = jnp.concatenate(
                        [values_t[h * head_size : (h + 1) * head_size], ones], axis=0
                    )
                    span = slice(side * points, (side + 1) * points)
                    added = jnp.dot(
                        with_ones, weights[:, span], preferred_element_type=jnp.float32
                    )
                    sums[image, h] = sums[image, h] * decay[:, span] + added * times

    for fetch in fetches:
        fetch.wait()
    images = range(img_count)
    messages = [
        jnp.concatenate(
            [
                sums[image, h, :head_size] / sums[image, h, head_size : head_size + 1]
                for h in range(HEADS)
            ],
            axis=0,
        ).T.astype(jnp.bfloat16)
        for image in images
    ]
    told = [
        jnp.dot(message, out_proj_ref[...], preferred_element_type=jnp.float32).astype(
            jnp.bfloat16
        )
        for message in messages
    ]
    hidden = [
        jnp.dot(own_ref[image], ffn_first_ref[:features], preferred_element_type=jnp.float32)
        + jnp.dot(told[image], ffn_first_ref[features:], preferred_element_type=jnp.float32)
        for image in images
    ]
    for image in images:
        centre = jnp.mean(hidden[image], axis=1, keepdims=True)
        deviation = hidden[image] - centre
        second_moment = jnp.mean(deviation * deviation, axis=1, keepdims=True)
        normed = deviation * lax.rsqrt(second_moment + 1e-05) * gain_ref[...] + bias_ref[...]
        active = 0.5 * normed * (1.0 + lax.erf(normed * math.sqrt(0.5)))
        result = own_ref[image].astype(jnp.float32) + jnp.dot(
            active.astype(jnp.bfloat16), ffn_second_ref[...], preferred_element_type=jnp.float32
        )
        out_ref[image] = result.astype(jnp.bfloat16)


def shards(
    device_count,
    descriptors,
    pair_list,
    key_proj,
    value_proj,
    out_proj,
    ffn_first,
    norm_gain,
    norm_bias,
    ffn_second,
):
    img_count, points, features = descriptors.shape
    slot_count = pair_list.shape[0]
    window = WINDOW * img_count
    in_vmem = pl.BlockSpec(memory_space=pltpu.VMEM)
    in_smem = pl.BlockSpec(memory_space=pltpu.SMEM)
    in_hbm = pl.BlockSpec(memory_space=pltpu.HBM)
    totals_shape = (img_count, HEADS, features // HEADS + ONES_ROWS, points)
    maxima_shape = (img_count, 8, 2 * points)
    keys, values, sums, maxima, lists = pl.pallas_call(
        functools.partial(exchange_kernel, device_count),
        out_shape=(
            jax.ShapeDtypeStruct((window, points, features), jnp.bfloat16),
            jax.ShapeDtypeStruct((window, features, points), jnp.bfloat16),
            jax.ShapeDtypeStruct(totals_shape, jnp.float32),
            jax.ShapeDtypeStruct(maxima_shape, jnp.float32),
            jax.ShapeDtypeStruct((REACH + 2, 2, 128), jnp.int32),
        ),
        in_specs=[in_hbm] * 4,
        out_specs=(in_hbm, in_hbm, in_hbm, in_hbm, in_vmem),
        scratch_shapes=[
            pltpu.VMEM(descriptors.shape, jnp.bfloat16),
            pltpu.VMEM(pair_list.shape[::-1], jnp.int32),
            pltpu.VMEM(key_proj.shape, jnp.bfloat16),
            pltpu.VMEM(value_proj.shape, jnp.bfloat16),
            pltpu.VMEM((window, points, features), jnp.bfloat16),
            pltpu.VMEM((window, features, points), jnp.bfloat16),
            pltpu.VMEM((4, img_count, points, features), jnp.bfloat16),
            pltpu.VMEM((5, 8, 128), jnp.int32),
            pltpu.VMEM((img_count, features, HEADS * points), jnp.bfloat16),
            pltpu.VMEM(totals_shape, jnp.float32),
            pltpu.VMEM(maxima_shape, jnp.float32),
            pltpu.SemaphoreType.DMA((4,)),
            pltpu.SemaphoreType.DMA((window, 2)),
            pltpu.SemaphoreType.DMA((2,)),
            pltpu.SemaphoreType.DMA((4, CHUNKS + 1)),
            pltpu.SemaphoreType.DMA((4, CHUNKS + 1)),
        ],
        compiler_params=pltpu.CompilerParams(
            collective_id=0, has_side_effects=True, vmem_limit_bytes=VMEM_BYTES
        ),
        name="exchange",
    )(descriptors, pair_list.T, key_proj, value_proj)
    return pl.pallas_call(
        functools.partial(attend_kernel, slot_count),
        out_shape=jax.ShapeDtypeStruct(descriptors.shape, jnp.bfloat16),
        in_specs=[in_smem] + [in_hbm] * 10,
        out_specs=in_vmem,
        scratch_shapes=[
            pltpu.VMEM(keys.shape, jnp.bfloat16),
            pltpu.VMEM(values.shape, jnp.bfloat16),
            pltpu.VMEM(descriptors.shape, jnp.bfloat16),
            pltpu.VMEM(out_proj.shape, jnp.bfloat16),
            pltpu.VMEM(ffn_first.shape, jnp.bfloat16),
            pltpu.VMEM((1,) + norm_gain.shape, jnp.float32),
            pltpu.VMEM((1,) + norm_bias.shape, jnp.float32),
            pltpu.VMEM(ffn_second.shape, jnp.bfloat16),
            pltpu.VMEM((img_count, features, HEADS * points), jnp.bfloat16),
            pltpu.VMEM(maxima_shape, jnp.float32),
            pltpu.VMEM(totals_shape, jnp.float32),
            pltpu.SMEM((img_count, window), jnp.int32),
            pltpu.SMEM((img_count, window + 1), jnp.int32),
            pltpu.SMEM((img_count,), jnp.int32),
            pltpu.SMEM((window,), jnp.int32),
            pltpu.SemaphoreType.DMA((2,)),
            pltpu.SemaphoreType.DMA((6,)),
            pltpu.SemaphoreType.DMA((window, 2)),
        ],
        compiler_params=pltpu.CompilerParams(vmem_limit_bytes=VMEM_BYTES),
        name="attend",
    )(
        lists,
        keys,
        values,
        sums,
        maxima,
        descriptors,
        out_proj,
        ffn_first,
        norm_gain.reshape(1, -1),
        norm_bias.reshape(1, -1),
        ffn_second,
    )


def solution(mesh):
    in_specs = (
        P(("groups", "img"), None, None),
        P(("groups", "img"), None),
        P(),
        P(),
        P(),
        P(),
        P(),
        P(),
        P(),
    )
    out_specs = P(("groups", "img"), None, None)
    return jax.shard_map(
        functools.partial(shards, mesh.shape["img"]),
        mesh=mesh,
        in_specs=in_specs,
        out_specs=out_specs,
        check_vma=False,
    )
```

```python
import functools
import math

import jax
import jax.numpy as jnp
from jax import lax
from jax.experimental import pallas as pl
from jax.experimental.pallas import tpu as pltpu
from jax.sharding import PartitionSpec as P

HEADS = 4
REACH = 2
WINDOW = 2 * REACH + 1
CHUNKS = 8
LAG = 3
FLOW_PARTNER, FLOW_FACING, FLOW_RELAY, FLOW_SHARED = range(4)
ONES_ROWS = 16
VERY_LOW = -1e30
VMEM_BYTES = 60 * 2**20


def project(rows, key_proj, value_proj_t):
    keys = jnp.dot(rows, key_proj, preferred_element_type=jnp.float32)
    values_t = lax.dot_general(
        value_proj_t, rows, (((1,), (1,)), ((), ())), preferred_element_type=jnp.float32
    )
    return keys.astype(jnp.bfloat16), values_t.astype(jnp.bfloat16)


def fill_queries(queries, keys):
    points, features = keys.shape
    head_size = features // HEADS
    head_of = lax.broadcasted_iota(jnp.int32, (features, points), 0) // head_size
    keys_t = keys.astype(jnp.float32).T * (1.0 / math.sqrt(head_size))
    for h in range(HEADS):
        queries[:, h * points : (h + 1) * points] = jnp.where(head_of == h, keys_t, 0.0).astype(
            jnp.bfloat16
        )


def exchange_kernel(
    device_count,
    own_hbm,
    pairs_hbm,
    key_proj_hbm,
    value_proj_hbm,
    keys_hbm,
    values_hbm,
    sums_hbm,
    maxima_hbm,
    lists_ref,
    own_ref,
    pairs_ref,
    key_proj_ref,
    value_proj_ref,
    keys_ref,
    values_ref,
    land,
    land_lists,
    queries,
    sums,
    maxima,
    fetch_sems,
    store_sems,
    state_sems,
    send_sems,
    recv_sems,
):
    img_count, points, features = own_hbm.shape
    me = lax.axis_index("img")
    chip = lax.div(me, 2)
    core = lax.rem(me, 2)
    odd = lax.rem(chip, 2)
    chip_count = device_count // 2
    partner = me + 1 - 2 * core
    facing = me + 2 * (1 - 2 * odd)
    relay_to = me + 4 * (1 - 2 * odd)
    relay_from = me - 4 * (1 - 2 * odd)
    gives_relay = (relay_to >= 0) & (relay_to < 2 * chip_count)
    gets_relay = (relay_from >= 0) & (relay_from < 2 * chip_count)
    shares_facing = odd == core
    shares_relay = (odd != core) & gets_relay
    gets_shared = (odd != core) | gets_relay

    fetches = [
        pltpu.make_async_copy(source, target, fetch_sems.at[index])
        for index, (source, target) in enumerate(
            (
                (pairs_hbm, pairs_ref),
                (own_hbm, own_ref),
                (key_proj_hbm, key_proj_ref),
                (value_proj_hbm, value_proj_ref),
            )
        )
    ]
    for fetch in fetches:
        fetch.start()
    land_lists[...] = jnp.full(land_lists.shape, -1, jnp.int32)

    barrier = pltpu.get_barrier_semaphore()

    def greet(device):
        pl.semaphore_signal(
            barrier, inc=1, device_id={"img": device}, device_id_type=pl.DeviceIdType.MESH
        )

    greet(partner)
    greet(facing)

    @pl.when(gives_relay)
    def _():
        greet(relay_to)

    @pl.when(gets_relay)
    def _():
        greet(relay_from)

    pl.semaphore_wait(
        barrier, 2 + gives_relay.astype(jnp.int32) + gets_relay.astype(jnp.int32)
    )

    pieces = CHUNKS // img_count
    rows = points // pieces

    def transfer(flow, part, source, device):
        if part == CHUNKS:
            src = land_lists.at[source]
            dst = land_lists.at[flow + 1]
        else:
            spot = (part // pieces, pl.ds((part % pieces) * rows, rows))
            src = own_hbm.at[spot] if source == 0 else land.at[(source - 1,) + spot]
            dst = land.at[(flow,) + spot]
        return pltpu.make_async_remote_copy(
            src_ref=src,
            dst_ref=dst,
            send_sem=send_sems.at[flow, part],
            recv_sem=recv_sems.at[flow, part],
            device_id={"img": device},
            device_id_type=pl.DeviceIdType.MESH,
        )

    parts = list(range(CHUNKS)) + [CHUNKS]
    for part in range(CHUNKS):
        transfer(FLOW_FACING, part, 0, facing).start()
    for part in range(CHUNKS):
        transfer(FLOW_PARTNER, part, 0, partner).start()
    fetches[0].wait()
    land_lists[0, 0 : pairs_ref.shape[0], 0 : pairs_ref.shape[1]] = pairs_ref[...]
    transfer(FLOW_FACING, CHUNKS, 0, facing).start()
    transfer(FLOW_PARTNER, CHUNKS, 0, partner).start()
    for fetch in fetches[1:]:
        fetch.wait()

    def after_facing(part):
        transfer(FLOW_FACING, part, 0, facing).wait_recv()

        @pl.when(gives_relay)
        def _():
            transfer(FLOW_RELAY, part, 1 + FLOW_FACING, relay_to).start()

        @pl.when(shares_facing)
        def _():
            transfer(FLOW_SHARED, part, 1 + FLOW_FACING, partner).start()

    def after_relay(part):
        @pl.when(gets_relay)
        def _():
            transfer(FLOW_RELAY, part, 1 + FLOW_FACING, relay_from).wait_recv()

        @pl.when(shares_relay)
        def _():
            transfer(FLOW_SHARED, part, 1 + FLOW_RELAY, partner).start()

    value_proj_t = value_proj_ref[...].T
    key_proj = key_proj_ref[...]

    def stores(slot, place, image):
        return [
            pltpu.make_async_copy(
                source.at[img_count * slot + image],
                target.at[img_count * place + image],
                store_sems.at[img_count * slot + image, index],
            )
            for index, (source, target) in enumerate(
                ((keys_ref, keys_hbm), (values_ref, values_hbm))
            )
        ]

    def project_image(slot, place, block_ref, image):
        keys, values_t = project(block_ref[image], key_proj, value_proj_t)
        keys_ref[img_count * slot + image] = keys
        values_ref[img_count * slot + image] = values_t
        for store in stores(slot, place, image):
            store.start()

    place_partner = REACH + 1 - 2 * core
    place_shared = REACH - 1 + 2 * core
    place_facing = 2 * REACH * (1 - odd)
    place_relay = 2 * REACH * odd

    def take_partner(image):
        for part in range(image * pieces, (image + 1) * pieces):
            transfer(FLOW_PARTNER, part, 0, partner).wait_recv()
        project_image(1 + FLOW_PARTNER, place_partner, land.at[FLOW_PARTNER], image)

    def take_relay(image):
        @pl.when(gets_relay)
        def _():
            project_image(1 + FLOW_RELAY, place_relay, land.at[FLOW_RELAY], image)

    def take_shared(image):
        @pl.when(gets_shared)
        def _():
            for part in range(image * pieces, (image + 1) * pieces):
                transfer(FLOW_SHARED, part, 1 + FLOW_FACING, partner).wait_recv()
            project_image(1 + FLOW_SHARED, place_shared, land.at[FLOW_SHARED], image)

    meanwhile = {}
    for image in range(img_count):
        meanwhile.setdefault(image, []).append(functools.partial(take_partner, image))
        if image + 1 < img_count:
            done = (image + 1) * pieces
            meanwhile.setdefault(done - 1, []).append(
                functools.partial(
                    project_image, 1 + FLOW_FACING, place_facing, land.at[FLOW_FACING], image
                )
            )
            meanwhile.setdefault(done - 1 + LAG, []).append(
                functools.partial(take_relay, image)
            )
            meanwhile.setdefault(done + LAG, []).append(functools.partial(take_shared, image))

    for image in range(img_count):
        project_image(0, REACH, own_ref, image)
    ones = jnp.ones((ONES_ROWS, points), jnp.bfloat16)
    head_size = features // HEADS
    for image in range(img_count):
        fill_queries(queries.at[image], keys_ref[image])
    sums[...] = jnp.zeros(sums.shape, jnp.float32)
    maxima[...] = jnp.full(maxima.shape, VERY_LOW, jnp.float32)

    def times_named(one, other, entries):
        total = jnp.zeros((1, 128), jnp.float32)
        for entry in entries:
            first = land_lists[entry, 0:1, :]
            second = land_lists[entry, 1:2, :]
            named = ((first == one) & (second == other)) | ((first == other) & (second == one))
            total = total + jnp.where(named, 1.0, 0.0)
        total = jnp.sum(total, axis=1, keepdims=True)
        return jnp.broadcast_to(total, (1, 2 * points))

    def near_scores(image, slot, source, pair):
        return jnp.dot(
            keys_ref[img_count * slot + source],
            queries[image, :, 2 * pair * points : 2 * (pair + 1) * points],
            preferred_element_type=jnp.float32,
        )

    def attend_near(scores, image, slot, source, pair):
        home = me if slot == 0 else partner
        times = times_named(
            me * img_count + image,
            home * img_count + source,
            (0,) if slot == 0 else (0, slot),
        )
        values_t = values_ref[img_count * slot + source]
        top = jnp.max(scores, axis=0, keepdims=True)
        weights = jnp.exp((scores - top).astype(jnp.bfloat16))
        held_max = maxima[image, pair : pair + 1]
        new_max = jnp.where(times > 0.0, jnp.maximum(held_max, top), held_max)
        decay = jnp.exp(held_max - new_max)
        share = times * jnp.exp(jnp.minimum(top - new_max, 0.0))
        maxima[image, pair : pair + 1] = new_max
        for side in range(2):
            h = 2 * pair + side
            with_ones = jnp.concatenate(
                [values_t[h * head_size : (h + 1) * head_size], ones], axis=0
            )
            span = slice(side * points, (side + 1) * points)
            added = jnp.dot(with_ones, weights[:, span], preferred_element_type=jnp.float32)
            sums[image, h] = sums[image, h] * decay[:, span] + added * share[:, span]

    near = [
        (image, slot, source, pair)
        for slot in (0, 1 + FLOW_PARTNER)
        for image in range(img_count)
        for source in range(img_count)
        if slot != 0 or source != image
        for pair in range(HEADS // 2)
    ]
    steps = CHUNKS + LAG
    ahead = near_scores(*near[0])

    def run_near(low, high):
        nonlocal ahead
        for index in range(low, min(high, len(near))):
            scores = ahead
            if index + 1 < len(near):
                ahead = near_scores(*near[index + 1])
            attend_near(scores, *near[index])

    run_near(0, len(near) // steps)
    for step in range(steps):
        if step < CHUNKS:
            after_facing(step)
        if step >= LAG:
            after_relay(step - LAG)
        if step == 0:
            transfer(FLOW_PARTNER, CHUNKS, 0, partner).wait_recv()
        for task in meanwhile.get(step, []):
            task()
        run_near((step + 1) * len(near) // steps, (step + 2) * len(near) // steps)
        if step == CHUNKS - 1:
            after_facing(CHUNKS)
            project_image(1 + FLOW_FACING, place_facing, land.at[FLOW_FACING], img_count - 1)
    state_stores = [
        pltpu.make_async_copy(sums, sums_hbm, state_sems.at[0]),
        pltpu.make_async_copy(maxima, maxima_hbm, state_sems.at[1]),
    ]
    for store in state_stores:
        store.start()
    after_relay(CHUNKS)
    take_relay(img_count - 1)
    take_shared(img_count - 1)

    @pl.when(gets_shared)
    def _():
        transfer(FLOW_SHARED, CHUNKS, 1 + FLOW_FACING, partner).wait_recv()

    for part in parts:
        transfer(FLOW_FACING, part, 0, facing).wait_send()
        transfer(FLOW_PARTNER, part, 0, partner).wait_send()

        @pl.when(gives_relay)
        def _():
            transfer(FLOW_RELAY, part, 1 + FLOW_FACING, relay_to).wait_send()

        @pl.when(shares_facing)
        def _():
            transfer(FLOW_SHARED, part, 1 + FLOW_FACING, partner).wait_send()

        @pl.when(shares_relay)
        def _():
            transfer(FLOW_SHARED, part, 1 + FLOW_RELAY, partner).wait_send()

    for store in state_stores:
        store.wait()
    for image in range(img_count):
        for slot, place in (
            (0, REACH),
            (1 + FLOW_PARTNER, place_partner),
            (1 + FLOW_FACING, place_facing),
        ):
            for store in stores(slot, place, image):
                store.wait()

        @pl.when(gets_relay)
        def _():
            for store in stores(1 + FLOW_RELAY, place_relay, image):
                store.wait()

        @pl.when(gets_shared)
        def _():
            for store in stores(1 + FLOW_SHARED, place_shared, image):
                store.wait()

    behind_two = jnp.where(odd == 1, land_lists[1 + FLOW_FACING], land_lists[1 + FLOW_RELAY])
    behind_one = jnp.where(core == 1, land_lists[1 + FLOW_PARTNER], land_lists[1 + FLOW_SHARED])
    first_image = (me - REACH) * img_count
    for place, entries in enumerate((behind_two, behind_one, land_lists[0])):
        used_entries = entries[: lists_ref.shape[1]]
        lists_ref[place] = jnp.where(used_entries >= 0, used_entries - first_image, -1)
    lists_ref[REACH + 1] = jnp.full(lists_ref.shape[1:], place_partner, jnp.int32)


def attend_kernel(
    slot_count,
    lists_ref,
    keys_hbm,
    values_hbm,
    sums_hbm,
    maxima_hbm,
    own_hbm,
    out_proj_hbm,
    ffn_first_hbm,
    gain_hbm,
    bias_hbm,
    ffn_second_hbm,
    out_ref,
    keys_ref,
    values_ref,
    own_ref,
    out_proj_ref,
    ffn_first_ref,
    gain_ref,
    bias_ref,
    ffn_second_ref,
    queries,
    maxima,
    sums,
    repeats,
    sources,
    counts,
    arrived,
    state_sems,
    fetch_sems,
    load_sems,
):
    img_count, points, features = own_ref.shape
    head_size = features // HEADS
    window = keys_ref.shape[0]
    first_own = REACH * img_count

    fetches = [
        pltpu.make_async_copy(source, target, fetch_sems.at[index])
        for index, (source, target) in enumerate(
            (
                (own_hbm, own_ref),
                (out_proj_hbm, out_proj_ref),
                (ffn_first_hbm, ffn_first_ref),
                (gain_hbm, gain_ref),
                (bias_hbm, bias_ref),
                (ffn_second_hbm, ffn_second_ref),
            )
        )
    ]

    def loads(source):
        return [
            pltpu.make_async_copy(held.at[source], to.at[source], load_sems.at[source, index])
            for index, (held, to) in enumerate(((keys_hbm, keys_ref), (values_hbm, values_ref)))
        ]

    for local in range(img_count):
        loads(first_own + local)[0].start()
    state_loads = [
        pltpu.make_async_copy(sums_hbm, sums, state_sems.at[0]),
        pltpu.make_async_copy(maxima_hbm, maxima, state_sems.at[1]),
    ]
    for load in state_loads:
        load.start()

    for local in range(img_count):
        for source in range(window):
            repeats[local, source] = 0

    def note(image, source):
        wanted = (image >= first_own) & (image < first_own + img_count)

        @pl.when(wanted)
        def _():
            local = image - first_own
            repeats[local, source] = repeats[local, source] + 1

    for group in range(REACH + 1):
        for slot in range(slot_count):
            first = lists_ref[group, 0, slot]
            second = lists_ref[group, 1, slot]
            if group == REACH:
                note(first, second)
            note(second, first)

    for local in range(img_count):
        for other in range(img_count):
            repeats[local, first_own + other] = 0
            repeats[local, lists_ref[REACH + 1, 0, 0] * img_count + other] = 0

    for local in range(img_count):
        held = jnp.int32(0)
        for source in range(window):
            sources[local, held] = source
            held = held + (repeats[local, source] > 0).astype(jnp.int32)
        counts[local] = held

    for source in range(window):
        arrived[source] = 0
        if not first_own <= source < first_own + img_count:
            used = repeats[0, source]
            for local in range(1, img_count):
                used = used + repeats[local, source]

            @pl.when(used > 0)
            def _():
                for load in loads(source):
                    load.start()

    for fetch in fetches:
        fetch.start()
    for local in range(img_count):
        loads(first_own + local)[0].wait()

    ones = jnp.ones((ONES_ROWS, points), jnp.bfloat16)

    for image in range(img_count):
        fill_queries(queries.at[image], keys_ref[first_own + image])
    for load in state_loads:
        load.wait()

    @pl.loop(0, img_count)
    def _(image):
        @pl.loop(0, counts[image])
        def _(index):
            source = sources[image, index]

            @pl.when(arrived[source] == 0)
            def _():
                for load in loads(source):
                    load.wait()
                arrived[source] = 1

            times = repeats[image, source].astype(jnp.float32)
            keys = keys_ref[source]
            values_t = values_ref[source]
            all_scores = [
                jnp.dot(
                    keys,
                    queries[image, :, 2 * pair * points : 2 * (pair + 1) * points],
                    preferred_element_type=jnp.float32,
                )
                for pair in range(HEADS // 2)
            ]
            for pair, scores in enumerate(all_scores):
                held_max = maxima[image, pair : pair + 1]
                top = jnp.maximum(held_max, jnp.max(scores, axis=0, keepdims=True))
                weights = jnp.exp((scores - top).astype(jnp.bfloat16))
                decay = jnp.exp(held_max - top)
                maxima[image, pair : pair + 1] = top
                for side in range(2):
                    h = 2 * pair + side
                    with_ones = jnp.concatenate(
                        [values_t[h * head_size : (h + 1) * head_size], ones], axis=0
                    )
                    span = slice(side * points, (side + 1) * points)
                    added = jnp.dot(
                        with_ones, weights[:, span], preferred_element_type=jnp.float32
                    )
                    sums[image, h] = sums[image, h] * decay[:, span] + added * times

    for fetch in fetches:
        fetch.wait()
    images = range(img_count)
    messages = [
        jnp.concatenate(
            [
                sums[image, h, :head_size] / sums[image, h, head_size : head_size + 1]
                for h in range(HEADS)
            ],
            axis=0,
        ).T.astype(jnp.bfloat16)
        for image in images
    ]
    told = [
        jnp.dot(message, out_proj_ref[...], preferred_element_type=jnp.float32).astype(
            jnp.bfloat16
        )
        for message in messages
    ]
    hidden = [
        jnp.dot(own_ref[image], ffn_first_ref[:features], preferred_element_type=jnp.float32)
        + jnp.dot(told[image], ffn_first_ref[features:], preferred_element_type=jnp.float32)
        for image in images
    ]
    for image in images:
        centre = jnp.mean(hidden[image], axis=1, keepdims=True)
        deviation = hidden[image] - centre
        second_moment = jnp.mean(deviation * deviation, axis=1, keepdims=True)
        normed = deviation * lax.rsqrt(second_moment + 1e-05) * gain_ref[...] + bias_ref[...]
        active = 0.5 * normed * (1.0 + lax.erf(normed * math.sqrt(0.5)))
        result = own_ref[image].astype(jnp.float32) + jnp.dot(
            active.astype(jnp.bfloat16), ffn_second_ref[...], preferred_element_type=jnp.float32
        )
        out_ref[image] = result.astype(jnp.bfloat16)


def shards(
    device_count,
    descriptors,
    pair_list,
    key_proj,
    value_proj,
    out_proj,
    ffn_first,
    norm_gain,
    norm_bias,
    ffn_second,
):
    img_count, points, features = descriptors.shape
    slot_count = pair_list.shape[0]
    window = WINDOW * img_count
    in_vmem = pl.BlockSpec(memory_space=pltpu.VMEM)
    in_smem = pl.BlockSpec(memory_space=pltpu.SMEM)
    in_hbm = pl.BlockSpec(memory_space=pltpu.HBM)
    totals_shape = (img_count, HEADS, features // HEADS + ONES_ROWS, points)
    maxima_shape = (img_count, 8, 2 * points)
    keys, values, sums, maxima, lists = pl.pallas_call(
        functools.partial(exchange_kernel, device_count),
        out_shape=(
            jax.ShapeDtypeStruct((window, points, features), jnp.bfloat16),
            jax.ShapeDtypeStruct((window, features, points), jnp.bfloat16),
            jax.ShapeDtypeStruct(totals_shape, jnp.float32),
            jax.ShapeDtypeStruct(maxima_shape, jnp.float32),
            jax.ShapeDtypeStruct((REACH + 2, 2, 128), jnp.int32),
        ),
        in_specs=[in_hbm] * 4,
        out_specs=(in_hbm, in_hbm, in_hbm, in_hbm, in_vmem),
        scratch_shapes=[
            pltpu.VMEM(descriptors.shape, jnp.bfloat16),
            pltpu.VMEM(pair_list.shape[::-1], jnp.int32),
            pltpu.VMEM(key_proj.shape, jnp.bfloat16),
            pltpu.VMEM(value_proj.shape, jnp.bfloat16),
            pltpu.VMEM((window, points, features), jnp.bfloat16),
            pltpu.VMEM((window, features, points), jnp.bfloat16),
            pltpu.VMEM((4, img_count, points, features), jnp.bfloat16),
            pltpu.VMEM((5, 8, 128), jnp.int32),
            pltpu.VMEM((img_count, features, HEADS * points), jnp.bfloat16),
            pltpu.VMEM(totals_shape, jnp.float32),
            pltpu.VMEM(maxima_shape, jnp.float32),
            pltpu.SemaphoreType.DMA((4,)),
            pltpu.SemaphoreType.DMA((window, 2)),
            pltpu.SemaphoreType.DMA((2,)),
            pltpu.SemaphoreType.DMA((4, CHUNKS + 1)),
            pltpu.SemaphoreType.DMA((4, CHUNKS + 1)),
        ],
        compiler_params=pltpu.CompilerParams(
            collective_id=0, has_side_effects=True, vmem_limit_bytes=VMEM_BYTES
        ),
        name="exchange",
    )(descriptors, pair_list.T, key_proj, value_proj)
    return pl.pallas_call(
        functools.partial(attend_kernel, slot_count),
        out_shape=jax.ShapeDtypeStruct(descriptors.shape, jnp.bfloat16),
        in_specs=[in_smem] + [in_hbm] * 10,
        out_specs=in_vmem,
        scratch_shapes=[
            pltpu.VMEM(keys.shape, jnp.bfloat16),
            pltpu.VMEM(values.shape, jnp.bfloat16),
            pltpu.VMEM(descriptors.shape, jnp.bfloat16),
            pltpu.VMEM(out_proj.shape, jnp.bfloat16),
            pltpu.VMEM(ffn_first.shape, jnp.bfloat16),
            pltpu.VMEM((1,) + norm_gain.shape, jnp.float32),
            pltpu.VMEM((1,) + norm_bias.shape, jnp.float32),
            pltpu.VMEM(ffn_second.shape, jnp.bfloat16),
            pltpu.VMEM((img_count, features, HEADS * points), jnp.bfloat16),
            pltpu.VMEM(maxima_shape, jnp.float32),
            pltpu.VMEM(totals_shape, jnp.float32),
            pltpu.SMEM((img_count, window), jnp.int32),
            pltpu.SMEM((img_count, window + 1), jnp.int32),
            pltpu.SMEM((img_count,), jnp.int32),
            pltpu.SMEM((window,), jnp.int32),
            pltpu.SemaphoreType.DMA((2,)),
            pltpu.SemaphoreType.DMA((6,)),
            pltpu.SemaphoreType.DMA((window, 2)),
        ],
        compiler_params=pltpu.CompilerParams(vmem_limit_bytes=VMEM_BYTES),
        name="attend",
    )(
        lists,
        keys,
        values,
        sums,
        maxima,
        descriptors,
        out_proj,
        ffn_first,
        norm_gain.reshape(1, -1),
        norm_bias.reshape(1, -1),
        ffn_second,
    )


def solution(mesh):
    in_specs = (
        P(("groups", "img"), None, None),
        P(("groups", "img"), None),
        P(),
        P(),
        P(),
        P(),
        P(),
        P(),
        P(),
    )
    out_specs = P(("groups", "img"), None, None)
    return jax.shard_map(
        functools.partial(shards, mesh.shape["img"]),
        mesh=mesh,
        in_specs=in_specs,
        out_specs=out_specs,
        check_vma=False,
    )
```
